32 devices in a mesh: tm: 4 (over x, core), height: 8 (over z, y).
Axes of the slice: x: 2, y: 2, z: 4, core: 2. Of those that a mesh axis runs over, the one named last changes fastest.
Arguments:
- clip: bfloat16 [8, 32, 64, 256], P('tm', 'height'), may hold values from -6 to 6
- cotangent: bfloat16 [8, 32, 64, 256], P('tm', 'height'), may hold values from -6 to 6
- spatial_weight: bfloat16 [3, 3, 256, 256], replicated, may hold values from -0.125 to 0.125
- temporal_weight: bfloat16 [3, 256, 256], replicated, may hold values from -0.21875 to 0.21875
Outputs:
- output: bfloat16 [8, 32, 64, 256], P('tm', 'height')
- grad_clip: bfloat16 [8, 32, 64, 256], P('tm', 'height')
- grad_spatial: float32 [589824], P(('tm', 'height'))
- grad_temporal: float32 [196608], P(('tm', 'height'))
The draws below stay inside these ranges and needn't reach their ends.
All inputs are finite; a program needn't handle non-finite values.
Results may differ from the reference program's by a relative error of at most 0.0049.
Values may be sent and summed in bfloat16 or wider, within the bound.
A program may use at most 64 MiB of HBM per device.

```python
import math
import jax
import jax.numpy as jnp
from jax import lax

C = 256
W = 64
FRAMES = 8
HEIGHT = 32


def with_spikes(values, rng, source, target, shards_of, factor):
    def block_of(position):
        return (jnp.arange(values.shape[position]) // (values.shape[position] // shards_of)).reshape((-1,) + (1,) * (values.ndim - 1 - position))

    first = jax.random.permutation(rng, shards_of)[block_of(target)]
    second = (block_of(target) + shards_of // 2) % shards_of
    return jnp.where((block_of(source) == first) | (block_of(source) == second), factor * values, values)


def steps_of(key, dims, cuts, smallest, largest):
    loudness, own = 1.0, jax.random.fold_in(key, 6)
    for position, blocks in cuts:
        steps = jnp.exp(jax.random.uniform(jax.random.fold_in(own, position), (blocks,), jnp.float32, smallest / len(cuts), largest / len(cuts)))
        loudness = loudness * jnp.repeat(steps, dims[position] // blocks).reshape([-1 if axis == position else 1 for axis in range(len(dims))])
    return loudness


def scatter_about(own_key, dims, scale, bound, cuts=(), dtype=jnp.bfloat16):
    level = steps_of(own_key, dims, cuts, -0.22, 0.18) if cuts else 1.0
    array = jax.random.normal(own_key, dims, jnp.float32) * scale * level
    return jnp.minimum(jnp.maximum(array, -bound), bound).astype(dtype)


def gaussian_with(stream_key, shape, spread, bound, cuts, heavy, held_as=jnp.bfloat16):
    values = spread * jax.random.normal(stream_key, shape, jnp.float32)
    if cuts:
        values = values * steps_of(stream_key, shape, cuts, -0.22, 0.18)
    return jnp.clip(with_spikes(values, jax.random.fold_in(stream_key, 3), *heavy), -bound, bound).astype(held_as)


def setup_inputs(seed: int = 0) -> dict:
    key_list = jax.random.split(jax.random.key(seed), 5)
    return {
        "clip": gaussian_with(key_list[0], (FRAMES, HEIGHT, W, C), 1.0, 6.0, ((0, 4), (1, 8)), (1, 3, 8, 2.0)),
        "cotangent": scatter_about(key_list[1], (FRAMES, HEIGHT, W, C), 1.0, 6.0, ((0, 4), (1, 8))),
        "spatial_weight": scatter_about(key_list[2], (3, 3, C, C), (9 * C) ** -0.5, 0.125),
        "temporal_weight": scatter_about(key_list[3], (3, C, C), (3 * C) ** -0.5, 0.21875),
    }


EPSILON = 1e-06

def activate(values):
    scale_inv = lax.rsqrt(lax.optimization_barrier(jnp.mean(values * values, axis=-1, keepdims=True)) + EPSILON)
    return jax.nn.silu(values * scale_inv)

def flat_dot(left, weight):
    keep_shape = left.shape[:-1]
    result = jnp.dot(left.reshape(-1, left.shape[-1]), weight, preferred_element_type=jnp.float32)
    return result.reshape(keep_shape + (weight.shape[-1],))

def outer_sum(left, right):
    channels = left.shape[-1]
    return lax.dot_general(left.reshape(-1, channels), right.reshape(-1, channels), (((0,), (0,)), ((), ())), preferred_element_type=jnp.float32)

def reference(clip, cotangent, spatial_weight, temporal_weight):
    frame_count, row_count, col_count, channels = clip.shape
    clip_wide = clip.astype(jnp.float32)
    activated = activate(clip_wide).astype(jnp.bfloat16)
    padded = jnp.pad(activated, ((0, 0), (1, 1), (1, 1), (0, 0)))
    spatial = jnp.zeros(clip.shape, jnp.float32)
    for tap_row in range(3):
        for tap_col in range(3):
            spatial = spatial + flat_dot(padded[:, tap_row:tap_row + row_count, tap_col:tap_col + col_count], spatial_weight[tap_row, tap_col])
    middle = spatial.astype(jnp.bfloat16)
    history = jnp.pad(middle, ((2, 0), (0, 0), (0, 0), (0, 0)))
    temporal = jnp.zeros(clip.shape, jnp.float32)
    for time_lag in range(3):
        temporal = temporal + flat_dot(history[2 - time_lag:2 - time_lag + frame_count], temporal_weight[time_lag])
    output = (clip_wide + temporal).astype(jnp.bfloat16)
    future = jnp.pad(cotangent, ((0, 2), (0, 0), (0, 0), (0, 0)))
    grad_wide = jnp.zeros(clip.shape, jnp.float32)
    for time_lag in range(3):
        grad_wide = grad_wide + flat_dot(future[time_lag:time_lag + frame_count], temporal_weight[time_lag].T)
    grad_mid = grad_wide.astype(jnp.bfloat16)
    grad_temporal = jnp.stack([outer_sum(history[2 - time_lag:2 - time_lag + frame_count], cotangent) for time_lag in range(3)])
    terms = []
    for tap_row in range(3):
        for tap_col in range(3):
            terms.append(outer_sum(padded[:, tap_row:tap_row + row_count, tap_col:tap_col + col_count], grad_mid))
    grad_spatial = jnp.stack(terms)
    grad_pad = jnp.pad(grad_mid, ((0, 0), (1, 1), (1, 1), (0, 0)))
    grad_act = jnp.zeros(clip.shape, jnp.float32)
    for tap_row in range(3):
        for tap_col in range(3):
            grad_act = grad_act + flat_dot(grad_pad[:, 2 - tap_row:2 - tap_row + row_count, 2 - tap_col:2 - tap_col + col_count], spatial_weight[tap_row, tap_col].T)
    unused, pullback = jax.vjp(activate, clip_wide)
    grad_clip = (cotangent.astype(jnp.float32) + pullback(grad_act)[0]).astype(jnp.bfloat16)
    grad_scale = 1.0 / math.sqrt(frame_count * row_count * col_count)
    return (output, grad_clip, (grad_spatial * grad_scale).reshape(-1), (grad_temporal * grad_scale).reshape(-1))
```

```python
import functools
import math

import jax
import jax.numpy as jnp
from jax import lax
from jax.experimental import pallas as pl
from jax.experimental.pallas import tpu as pltpu
from jax.sharding import PartitionSpec as P

EPSILON = 1e-06
MESH = pl.DeviceIdType.MESH
F32 = jnp.float32
BF16 = jnp.bfloat16
NN = (((1,), (0,)), ((), ()))
NT = (((1,), (1,)), ((), ()))
TN = (((0,), (0,)), ((), ()))

SPATIAL_ROWS = 72
TEMPORAL_ROWS = 24
SLICE_ROWS = SPATIAL_ROWS + TEMPORAL_ROWS
HALF = SLICE_ROWS // 2


def dot(left, right, dims=NN):
    return lax.dot_general(left, right, dims, preferred_element_type=F32)


def flat(block):
    return block.reshape(-1, block.shape[-1])


def activate(values):
    scale_inv = lax.rsqrt(jnp.mean(values * values, axis=-1, keepdims=True) + EPSILON)
    normed = values * scale_inv
    return normed / (1.0 + jnp.exp(-normed))


def columns(block):
    wide = block.astype(F32)
    zero = jnp.zeros(wide.shape[:-2] + (1,) + wide.shape[-1:], F32)
    axis = wide.ndim - 2
    count = wide.shape[axis]
    before = jnp.concatenate([zero, lax.slice_in_dim(wide, 0, count - 1, axis=axis)], axis=axis)
    after = jnp.concatenate([lax.slice_in_dim(wide, 1, count, axis=axis), zero], axis=axis)
    return before.astype(BF16), block.astype(BF16), after.astype(BF16)


def body(
    sizes, reduce_inside, clip, cot, sw, tw, out, gclip, gs_out, gt_out,
    clip_halo, cot_next, mid_prev, mid, gm, gm_halo, act3, gm3, gmx, gs, gt, hsend, hrecv, *rest
):
    tm_count, h_count = sizes
    frames, rows, cols, ch = clip.shape
    tm = lax.axis_index("tm")
    hh = lax.axis_index("height")
    cells = rows * cols

    up, down = {"height": hh - 1}, {"height": hh + 1}
    before, after = {"tm": tm - 1}, {"tm": tm + 1}
    has_up, has_down = hh > 0, hh < h_count - 1
    has_before, has_after = tm > 0, tm < tm_count - 1

    barrier = pltpu.get_barrier_semaphore()

    def greet(where, who):
        @pl.when(where)
        def _():
            pl.semaphore_signal(barrier, inc=1, device_id=who, device_id_type=MESH)

    sides = ((has_up, up), (has_down, down), (has_before, before), (has_after, after))
    for where, who in sides:
        greet(where, who)
    if reduce_inside:
        core, xx, yy, zz = lax.rem(tm, 2), tm // 2, lax.rem(hh, 2), hh // 2
        by_core = {"tm": xx * 2 + 1 - core}
        by_x = {"tm": (1 - xx) * 2 + core}
        by_y = {"height": zz * 2 + 1 - yy}
        by_z = [{"height": lax.rem(zz + off, 4) * 2 + yy} for off in (1, 2, 3)]
        for who in [by_core, by_x, by_y] + by_z:
            pl.semaphore_signal(barrier, inc=1, device_id=who, device_id_type=MESH)

    greeted = 6 if reduce_inside else 0
    for where, who in sides:
        greeted = greeted + where.astype(jnp.int32)
    pl.semaphore_wait(barrier, greeted)

    def copy(src, dst, slot, who):
        return pltpu.make_async_remote_copy(
            src_ref=src, dst_ref=dst, send_sem=hsend.at[slot], recv_sem=hrecv.at[slot],
            device_id=who, device_id_type=MESH,
        )

    def exchange(slot, src_first, src_last, dst, send_up, send_down):
        return (
            (copy(src_first, dst.at[1], slot, up), has_up, has_down),
            (copy(src_last, dst.at[0], slot + 1, down), has_down, has_up),
        )

    def start(c):
        @pl.when(c[1])
        def _():
            c[0].start()

    def wait_recv(c, target):
        @pl.when(c[2])
        def _():
            c[0].wait_recv()

        @pl.when(jnp.logical_not(c[2]))
        def _():
            target[...] = jnp.zeros(target.shape, target.dtype)

    def wait_send(c):
        @pl.when(c[1])
        def _():
            c[0].wait_send()

    cot_copy = (copy(cot, cot_next, 0, before), has_before, has_after)
    clip_up, clip_down = exchange(1, clip.at[:, 0], clip.at[:, rows - 1], clip_halo, up, down)
    start(clip_up)
    start(clip_down)
    start(cot_copy)

    zero_edge = jnp.zeros((frames, 1, cols, ch), BF16)
    for r in range(3):
        lanes = pl.ds(r * ch, ch)
        for row in range(rows + 2):
            if not r <= row < r + rows:
                gmx[:, row : row + 1, :, lanes] = zero_edge

    def put_act(f, row, values):
        act = activate(values.astype(F32))
        for q, part in enumerate(columns(act)):
            act3[f, row, :, pl.ds(q * ch, ch)] = part

    for f in range(frames):
        for row in range(rows):
            put_act(f, row + 1, clip[f, row])
    wait_recv(clip_up, clip_halo.at[1])
    wait_recv(clip_down, clip_halo.at[0])
    for f in range(frames):
        put_act(f, 0, clip_halo[0, f])
        put_act(f, rows + 1, clip_halo[1, f])

    for f in range(frames):
        total = None
        for r in range(3):
            term = dot(flat(act3[f, r : r + rows]), flat(sw[r]))
            total = term if total is None else total + term
        mid[f] = total.astype(BF16).reshape(rows, cols, ch)
    mid_copy = (copy(mid, mid_prev, 3, after), has_after, has_before)
    start(mid_copy)

    wait_recv(cot_copy, cot_next)

    def future(t):
        return cot[t] if t < frames else cot_next[t - frames]

    for f in range(frames):
        total = None
        for k in range(3):
            term = dot(flat(future(f + k)), tw[k], NT)
            total = term if total is None else total + term
        value = total.astype(BF16).reshape(rows, cols, ch)
        gm[f] = value
        for r in range(3):
            gmx[f, r : r + rows, :, pl.ds(r * ch, ch)] = value
    gm_up, gm_down = exchange(4, gm.at[:, 0], gm.at[:, rows - 1], gm_halo, up, down)
    start(gm_up)
    start(gm_down)

    wide = frames * (rows + 2) * cols
    for q in range(3):
        left = act3[:, :, :, pl.ds(q * ch, ch)].reshape(wide, ch)
        for r in range(3):
            right = gmx[:, :, :, pl.ds(r * ch, ch)].reshape(wide, ch)
            gs[pl.ds((r * 3 + q) * ch, ch), :] = dot(left, right, TN)

    wait_recv(mid_copy, mid_prev)

    def history(t):
        return mid[t] if t >= 0 else mid_prev[frames + t]

    for k in range(3):
        total = None
        for f in range(frames):
            term = dot(flat(history(f - k)), flat(cot[f]), TN)
            total = term if total is None else total + term
        gt[pl.ds(k * ch, ch), :] = total

    def do_output(f):
        total = flat(clip[f]).astype(F32)
        for k in range(3):
            total = total + dot(flat(history(f - k)), tw[k])
        out[f] = total.astype(BF16).reshape(rows, cols, ch)

    def do_gm3():
        wait_recv(gm_up, gm_halo.at[1])
        wait_recv(gm_down, gm_halo.at[0])
        for f in range(frames):
            for row in range(rows + 2):
                if row == 0:
                    value = gm_halo[0, f]
                elif row == rows + 1:
                    value = gm_halo[1, f]
                else:
                    value = gm[f, row - 1]
                shifts = columns(value)
                for q in range(3):
                    gm3[f, row, :, pl.ds(q * ch, ch)] = shifts[2 - q]

    def do_grad_clip(f):
        total = None
        for r in range(3):
            for q in range(3):
                left = flat(gm3[f, 2 - r : 2 - r + rows, :, pl.ds(q * ch, ch)])
                term = dot(left, sw[r, q], NT)
                total = term if total is None else total + term
        values = flat(clip[f]).astype(F32)
        scale_inv = lax.rsqrt(jnp.mean(values * values, axis=-1, keepdims=True) + EPSILON)
        normed = values * scale_inv
        gate = 1.0 / (1.0 + jnp.exp(-normed))
        inner = total * (gate * (1.0 + normed * (1.0 - gate)))
        slope = scale_inv * (inner - normed * jnp.mean(inner * normed, axis=-1, keepdims=True))
        gclip[f] = (flat(cot[f]).astype(F32) + slope).astype(BF16).reshape(rows, cols, ch)

    scale = 1.0 / math.sqrt(frames * tm_count * rows * h_count * cols)

    if not reduce_inside:
        for f in range(frames):
            do_output(f)
        do_gm3()
        for f in range(frames):
            do_grad_clip(f)
        gs_out[...] = gs[...] * scale
        gt_out[...] = gt[...] * scale
    else:
        (send0, recv0, part, send_a1, recv_a1, send_b1, recv_b1, send_a2, recv_a2, send_b2, recv_b2,
         send_z, recv_z, total_z, rsend, rrecv) = rest

        def rcopy(src, dst, slot, who):
            return pltpu.make_async_remote_copy(
                src_ref=src, dst_ref=dst, send_sem=rsend.at[slot], recv_sem=rrecv.at[slot],
                device_id=who, device_id_type=MESH,
            )

        def slice_of(d):
            top = gs[pl.ds(pl.multiple_of(d * SPATIAL_ROWS, 8), SPATIAL_ROWS), :]
            low = gt[pl.ds(pl.multiple_of(d * TEMPORAL_ROWS, 8), TEMPORAL_ROWS), :]
            return jnp.concatenate([top, low], axis=0)

        def each(count):
            def run(step):
                lax.fori_loop(0, count, lambda j, carry: (step(j), carry)[1], 0)
            return run

        @each(16)
        def _(j):
            send0[j] = slice_of(((j // 8) * 2 + 1 - core) * 8 + lax.rem(j, 8)).astype(BF16)

        c0 = rcopy(send0, recv0, 0, by_core)
        c0.start()
        do_output(0)
        do_gm3()
        c0.wait()

        @each(16)
        def _(j):
            own = slice_of(((j // 8) * 2 + core) * 8 + lax.rem(j, 8))
            part[j] = own + recv0[j].astype(F32)

        @each(8)
        def _(j):
            send_a1[j] = part[(1 - xx) * 8 + j, :HALF].astype(BF16)
            send_b1[j] = part[j * 2 + 1 - yy, HALF:].astype(BF16)

        ca = rcopy(send_a1, recv_a1, 1, by_x)
        cb = rcopy(send_b1, recv_b1, 2, by_y)
        ca.start()
        cb.start()
        do_grad_clip(0)
        ca.wait()
        cb.wait()

        @each(8)
        def _(j):
            here = xx * 8 + j
            part[here, :HALF] = part[here, :HALF] + recv_a1[j].astype(F32)
            there = j * 2 + yy
            part[there, HALF:] = part[there, HALF:] + recv_b1[j].astype(F32)

        @each(4)
        def _(j):
            send_a2[j] = part[xx * 8 + j * 2 + 1 - yy, :HALF].astype(BF16)
            send_b2[j] = part[(1 - xx) * 8 + j * 2 + yy, HALF:].astype(BF16)

        ca2 = rcopy(send_a2, recv_a2, 3, by_y)
        cb2 = rcopy(send_b2, recv_b2, 4, by_x)
        ca2.start()
        cb2.start()
        do_output(1)
        ca2.wait()
        cb2.wait()

        @each(4)
        def _(j):
            place = xx * 8 + j * 2 + yy
            value = part[place] + jnp.concatenate(
                [recv_a2[j].astype(F32), recv_b2[j].astype(F32)], axis=0
            )
            total_z[j] = value
            send_z[j] = value.astype(BF16)

        cz = [
            rcopy(send_z.at[lax.rem(zz + off, 4)], recv_z.at[off - 1], 4 + off, by_z[off - 1])
            for off in (1, 2, 3)
        ]
        for c in cz:
            c.start()
        do_grad_clip(1)
        for c in cz:
            c.wait()
        value = total_z[zz]
        for off in range(3):
            value = value + recv_z[off].astype(F32)
        value = value * scale
        gs_out[...] = value[:SPATIAL_ROWS]
        gt_out[...] = value[SPATIAL_ROWS:]

    for c in (clip_up, clip_down, cot_copy, mid_copy, gm_up, gm_down):
        wait_send(c)


def shards(sizes, clip, cot, sw, tw):
    tm_count, h_count = sizes
    frames, rows, cols, ch = clip.shape
    inside = sizes == (4, 8) and ch == 256 and frames == 2
    wide = (frames, rows + 2, cols, 3 * ch)
    edge = (2, frames, cols, ch)
    vmem = pl.BlockSpec(memory_space=pltpu.VMEM)
    scratch = [
        pltpu.VMEM(edge, BF16),
        pltpu.VMEM(clip.shape, BF16),
        pltpu.VMEM(clip.shape, BF16),
        pltpu.VMEM(clip.shape, BF16),
        pltpu.VMEM(clip.shape, BF16),
        pltpu.VMEM(edge, BF16),
        pltpu.VMEM(wide, BF16),
        pltpu.VMEM(wide, BF16),
        pltpu.VMEM(wide, BF16),
        pltpu.VMEM((9 * ch, ch), F32),
        pltpu.VMEM((3 * ch, ch), F32),
        pltpu.SemaphoreType.DMA((6,)),
        pltpu.SemaphoreType.DMA((6,)),
    ]
    gs_shape, gt_shape = (9 * ch, ch), (3 * ch, ch)
    if inside:
        gs_shape, gt_shape = (SPATIAL_ROWS, ch), (TEMPORAL_ROWS, ch)
        scratch += [
            pltpu.VMEM((16, SLICE_ROWS, ch), BF16),
            pltpu.VMEM((16, SLICE_ROWS, ch), BF16),
            pltpu.VMEM((16, SLICE_ROWS, ch), F32),
        ]
        scratch += [pltpu.VMEM((8, HALF, ch), BF16)] * 4
        scratch += [pltpu.VMEM((4, HALF, ch), BF16)] * 4
        scratch += [
            pltpu.VMEM((4, SLICE_ROWS, ch), BF16),
            pltpu.VMEM((3, SLICE_ROWS, ch), BF16),
            pltpu.VMEM((4, SLICE_ROWS, ch), F32),
            pltpu.SemaphoreType.DMA((8,)),
            pltpu.SemaphoreType.DMA((8,)),
        ]
    out, gclip, gs, gt = pl.pallas_call(
        functools.partial(body, sizes, inside),
        out_shape=(
            jax.ShapeDtypeStruct(clip.shape, BF16),
            jax.ShapeDtypeStruct(clip.shape, BF16),
            jax.ShapeDtypeStruct(gs_shape, F32),
            jax.ShapeDtypeStruct(gt_shape, F32),
        ),
        in_specs=[vmem] * 4,
        out_specs=(vmem,) * 4,
        scratch_shapes=scratch,
        compiler_params=pltpu.CompilerParams(
            collective_id=0, has_side_effects=True, vmem_limit_bytes=48 * 1024 * 1024
        ),
        name="section",
    )(clip, cot, sw, tw)
    gs, gt = gs.reshape(-1), gt.reshape(-1)
    if not inside:
        gs, gt = (
            lax.psum_scatter(gs, ("tm", "height"), scatter_dimension=0, tiled=True),
            lax.psum_scatter(gt, ("tm", "height"), scatter_dimension=0, tiled=True),
        )
    return out, gclip, gs, gt


def solution(mesh):
    sizes = (mesh.shape["tm"], mesh.shape["height"])
    return jax.shard_map(
        functools.partial(shards, sizes),
        mesh=mesh,
        in_specs=(P("tm", "height", None, None), P("tm", "height", None, None), P(), P()),
        out_specs=(
            P("tm", "height", None, None),
            P("tm", "height", None, None),
            P(("tm", "height")),
            P(("tm", "height")),
        ),
        check_vma=False,
    )
```

```python
import functools
import math

import jax
import jax.numpy as jnp
from jax import lax
from jax.experimental import pallas as pl
from jax.experimental.pallas import tpu as pltpu
from jax.sharding import PartitionSpec as P

EPSILON = 1e-06
MESH = pl.DeviceIdType.MESH
F32 = jnp.float32
BF16 = jnp.bfloat16
NN = (((1,), (0,)), ((), ()))
NT = (((1,), (1,)), ((), ()))
TN = (((0,), (0,)), ((), ()))

SPATIAL_ROWS = 72
TEMPORAL_ROWS = 24
LANES = 128
CHUNKS = (("spatial", 0, 32, 32), ("spatial", 64, 32, 48), ("temporal", 0, 32, 16))


def dot(left, right, dims=NN):
    return lax.dot_general(left, right, dims, preferred_element_type=F32)


def flat(block):
    return block.reshape(-1, block.shape[-1])


def activate(values):
    scale_inv = lax.rsqrt(jnp.mean(values * values, axis=-1, keepdims=True) + EPSILON)
    normed = values * scale_inv
    return normed / (1.0 + jnp.exp(-normed))


def columns(block):
    wide = block.astype(F32)
    zero = jnp.zeros(wide.shape[:-2] + (1,) + wide.shape[-1:], F32)
    axis = wide.ndim - 2
    count = wide.shape[axis]
    before = jnp.concatenate([zero, lax.slice_in_dim(wide, 0, count - 1, axis=axis)], axis=axis)
    after = jnp.concatenate([lax.slice_in_dim(wide, 1, count, axis=axis), zero], axis=axis)
    return before.astype(BF16), block.astype(BF16), after.astype(BF16)


def body(
    sizes, reduce_inside, clip_hbm, cot_hbm, sw_hbm, tw_hbm, out_hbm, gclip_hbm, gs_out, gt_out,
    clip, cot, sw, tw, out, gclip, in_sem, out_sem,
    clip_halo, cot_next, mid_prev, mid, gm, gm_halo, act3, gm3, act_t, gs, gt, hsend, hrecv, *rest
):
    tm_count, h_count = sizes
    frames, rows, cols, ch = clip.shape
    tm = lax.axis_index("tm")
    hh = lax.axis_index("height")
    cells = rows * cols

    loads = [
        pltpu.make_async_copy(src, dst, in_sem.at[i])
        for i, (src, dst) in enumerate(
            ((clip_hbm, clip), (cot_hbm, cot), (sw_hbm, sw), (tw_hbm, tw))
        )
    ]
    for load in loads:
        load.start()

    up, down = {"height": hh - 1}, {"height": hh + 1}
    before, after = {"tm": tm - 1}, {"tm": tm + 1}
    has_up, has_down = hh > 0, hh < h_count - 1
    has_before, has_after = tm > 0, tm < tm_count - 1

    barrier = pltpu.get_barrier_semaphore()

    def greet(where, who):
        @pl.when(where)
        def _():
            pl.semaphore_signal(barrier, inc=1, device_id=who, device_id_type=MESH)

    sides = ((has_up, up), (has_down, down), (has_before, before), (has_after, after))
    for where, who in sides:
        greet(where, who)
    if reduce_inside:
        core, xx, yy, zz = lax.rem(tm, 2), tm // 2, lax.rem(hh, 2), hh // 2
        by_core = {"tm": xx * 2 + 1 - core}
        by_x = {"tm": (1 - xx) * 2 + core}
        by_y = {"height": zz * 2 + 1 - yy}
        by_z = [{"height": lax.rem(zz + off, 4) * 2 + yy} for off in (1, 2, 3)]
        for who in [by_core, by_x, by_y] + by_z:
            pl.semaphore_signal(barrier, inc=1, device_id=who, device_id_type=MESH)

    greeted = 6 if reduce_inside else 0
    for where, who in sides:
        greeted = greeted + where.astype(jnp.int32)
    pl.semaphore_wait(barrier, greeted)

    def copy(src, dst, slot, who):
        return pltpu.make_async_remote_copy(
            src_ref=src, dst_ref=dst, send_sem=hsend.at[slot], recv_sem=hrecv.at[slot],
            device_id=who, device_id_type=MESH,
        )

    def exchange(slot, src_first, src_last, dst, send_up, send_down):
        return (
            (copy(src_first, dst.at[1], slot, up), has_up, has_down),
            (copy(src_last, dst.at[0], slot + 1, down), has_down, has_up),
        )

    def start(c):
        @pl.when(c[1])
        def _():
            c[0].start()

    def wait_recv(c, target):
        @pl.when(c[2])
        def _():
            c[0].wait_recv()

        @pl.when(jnp.logical_not(c[2]))
        def _():
            target[...] = jnp.zeros(target.shape, target.dtype)

    def wait_send(c):
        @pl.when(c[1])
        def _():
            c[0].wait_send()

    cot_copy = (copy(cot_hbm, cot_next, 0, before), has_before, has_after)
    clip_up, clip_down = exchange(1, clip_hbm.at[:, 0], clip_hbm.at[:, rows - 1], clip_halo, up, down)
    start(clip_up)
    start(clip_down)
    start(cot_copy)

    loads[0].wait()

    def put_act(f, row, values):
        act = activate(values.astype(F32))
        for q, part in enumerate(columns(act)):
            act3[f, row, :, pl.ds(q * ch, ch)] = part

    for f in range(frames):
        for row in range(rows):
            put_act(f, row + 1, clip[f, row])
    wait_recv(clip_up, clip_halo.at[1])
    wait_recv(clip_down, clip_halo.at[0])
    for f in range(frames):
        put_act(f, 0, clip_halo[0, f])
        put_act(f, rows + 1, clip_halo[1, f])

    loads[2].wait()
    for f in range(frames):
        total = None
        for r in range(3):
            term = dot(flat(act3[f, r : r + rows]), flat(sw[r]))
            total = term if total is None else total + term
        mid[f] = total.astype(BF16).reshape(rows, cols, ch)
    mid_copy = (copy(mid, mid_prev, 3, after), has_after, has_before)
    start(mid_copy)

    for r in range(3):
        for f in range(frames):
            act_t[r, :, pl.ds(f * cells, cells)] = flat(
                act3[f, r : r + rows, :, pl.ds(ch, ch)]
            ).T

    loads[1].wait()
    loads[3].wait()
    wait_recv(cot_copy, cot_next)

    def put_gm(f, row, values):
        shifts = columns(values)
        for q in range(3):
            gm3[f, row, :, pl.ds(q * ch, ch)] = shifts[2 - q]

    def future(t):
        return cot[t] if t < frames else cot_next[t - frames]

    for f in range(frames):
        total = None
        for k in range(3):
            term = dot(flat(future(f + k)), tw[k], NT)
            total = term if total is None else total + term
        value = total.astype(BF16).reshape(rows, cols, ch)
        gm[f] = value
        for row in range(rows):
            put_gm(f, row + 1, value[row])
    gm_up, gm_down = exchange(4, gm.at[:, 0], gm.at[:, rows - 1], gm_halo, up, down)
    start(gm_up)
    start(gm_down)

    for r in range(3):
        total = None
        for f in range(frames):
            term = dot(
                act_t[r, :, pl.ds(f * cells, cells)], flat(gm3[f, 1 : 1 + rows])
            )
            total = term if total is None else total + term
        for q in range(3):
            gs[pl.ds((r * 3 + q) * ch, ch), :] = total[:, q * ch : (q + 1) * ch]

    def history(t):
        return mid[t] if t >= 0 else mid_prev[frames + t]

    def do_temporal():
        wait_recv(mid_copy, mid_prev)
        turned = {t: flat(history(t)).T for t in range(-2, frames)}
        for k in range(3):
            total = None
            for f in range(frames):
                term = dot(turned[f - k], flat(cot[f]))
                total = term if total is None else total + term
            gt[pl.ds(k * ch, ch), :] = total

    stores = []

    def store(src, dst, f, slot):
        c = pltpu.make_async_copy(src.at[f], dst.at[f], out_sem.at[slot])
        c.start()
        stores.append(c)

    def do_output(f):
        total = flat(clip[f]).astype(F32)
        for k in range(3):
            total = total + dot(flat(history(f - k)), tw[k])
        out[f] = total.astype(BF16).reshape(rows, cols, ch)
        store(out, out_hbm, f, f)

    def do_gm_halo():
        wait_recv(gm_up, gm_halo.at[1])
        wait_recv(gm_down, gm_halo.at[0])
        for f in range(frames):
            put_gm(f, 0, gm_halo[0, f])
            put_gm(f, rows + 1, gm_halo[1, f])

    def do_grad_clip(f):
        total = None
        for r in range(3):
            for q in range(3):
                left = flat(gm3[f, 2 - r : 2 - r + rows, :, pl.ds(q * ch, ch)])
                term = dot(left, sw[r, q], NT)
                total = term if total is None else total + term
        values = flat(clip[f]).astype(F32)
        scale_inv = lax.rsqrt(jnp.mean(values * values, axis=-1, keepdims=True) + EPSILON)
        normed = values * scale_inv
        gate = 1.0 / (1.0 + jnp.exp(-normed))
        inner = total * (gate * (1.0 + normed * (1.0 - gate)))
        slope = scale_inv * (inner - normed * jnp.mean(inner * normed, axis=-1, keepdims=True))
        gclip[f] = (flat(cot[f]).astype(F32) + slope).astype(BF16).reshape(rows, cols, ch)
        store(gclip, gclip_hbm, f, frames + f)

    scale = 1.0 / math.sqrt(frames * tm_count * rows * h_count * cols)

    if not reduce_inside:
        do_temporal()
        for f in range(frames):
            do_output(f)
        do_gm_halo()
        for f in range(frames):
            do_grad_clip(f)
        gs_out[...] = gs[...] * scale
        gt_out[...] = gt[...] * scale
    else:
        rsend, rrecv = rest[-2:]
        bufs = [rest[11 * i : 11 * i + 11] for i in range(len(CHUNKS))]

        def rcopy(src, dst, slot, who):
            return pltpu.make_async_remote_copy(
                src_ref=src, dst_ref=dst, send_sem=rsend.at[slot], recv_sem=rrecv.at[slot],
                device_id=who, device_id_type=MESH,
            )

        def piece(chunk, d):
            kind, first, a, b = chunk
            ref, count = (gs, SPATIAL_ROWS) if kind == "spatial" else (gt, TEMPORAL_ROWS)
            block = ref[pl.ds(pl.multiple_of(d * count, 8), count), :]
            both = jnp.concatenate([block[:, :LANES], block[:, LANES:]], axis=0)
            return both[first : first + a + b]

        def each(count):
            def run(step):
                def four(j, carry):
                    for i in range(4):
                        step(j * 4 + i)
                    return carry

                lax.fori_loop(0, count // 4, four, 0)

            return run

        def owner(j, which):
            return ((j // 8) * 2 + which) * 8 + lax.rem(j, 8)

        def stage_core(i):
            send0, recv0 = bufs[i][:2]

            @each(16)
            def _(j):
                send0[j] = piece(CHUNKS[i], owner(j, 1 - core)).astype(BF16)

            c = rcopy(send0, recv0, 8 * i, by_core)
            c.start()
            return [c]

        def stage_one(i):
            a = CHUNKS[i][2]
            send0, recv0, part, send_a, recv_a, send_b, recv_b = bufs[i][:7]

            @each(16)
            def _(j):
                part[j] = piece(CHUNKS[i], owner(j, core)) + recv0[j].astype(F32)

            @each(8)
            def _(j):
                send_a[j] = part[(1 - xx) * 8 + j, :a].astype(BF16)
                send_b[j] = part[j * 2 + 1 - yy, a:].astype(BF16)

            cs = [
                rcopy(send_a, recv_a, 8 * i + 1, by_x),
                rcopy(send_b, recv_b, 8 * i + 2, by_y),
            ]
            for c in cs:
                c.start()
            return cs

        def stage_two(i):
            a = CHUNKS[i][2]
            part, _, recv_a, _, recv_b, send_a2, recv_a2, send_b2, recv_b2 = bufs[i][2:11]

            @each(4)
            def _(j):
                away = j * 2 + 1 - yy
                send_a2[j] = (part[xx * 8 + away, :a] + recv_a[away].astype(F32)).astype(BF16)
                far = (1 - xx) * 4 + j
                send_b2[j] = (part[far * 2 + yy, a:] + recv_b[far].astype(F32)).astype(BF16)

            cs = [
                rcopy(send_a2, recv_a2, 8 * i + 3, by_y),
                rcopy(send_b2, recv_b2, 8 * i + 4, by_x),
            ]
            for c in cs:
                c.start()
            return cs

        z_bufs = rest[11 * len(CHUNKS) : -2]

        def stage_z(i):
            a = CHUNKS[i][2]
            part, _, recv_a, _, recv_b, _, recv_a2, _, recv_b2 = bufs[i][2:11]
            total_z, send_z, recv_z = z_bufs[3 * i : 3 * i + 3]

            @each(4)
            def _(j):
                near = j * 2 + yy
                first = part[xx * 8 + near, :a] + recv_a[near].astype(F32) + recv_a2[j].astype(F32)
                last = (
                    part[xx * 8 + near, a:] + recv_b[xx * 4 + j].astype(F32) + recv_b2[j].astype(F32)
                )
                value = jnp.concatenate([first, last], axis=0)
                total_z[j] = value
                send_z[j] = value.astype(BF16)

            cs = [
                rcopy(
                    send_z.at[lax.rem(zz + off, 4)], recv_z.at[off - 1], 8 * i + 4 + off, by_z[off - 1]
                )
                for off in (1, 2, 3)
            ]
            for c in cs:
                c.start()
            return cs

        def final(i):
            total_z, _, recv_z = z_bufs[3 * i : 3 * i + 3]
            value = total_z[zz]
            for off in range(3):
                value = value + recv_z[off].astype(F32)
            return value * scale

        def finish(copies):
            for c in copies:
                c.wait()

        def place(ref, value, count):
            ref[pl.ds(0, count, stride=2), :] = value[:count]
            ref[pl.ds(1, count, stride=2), :] = value[count:]

        spatial = (0, 1)
        flight = {i: stage_core(i) for i in spatial}
        do_temporal()
        flight[2] = stage_core(2)

        def advance(stage):
            for i in range(len(CHUNKS)):
                finish(flight[i])
                flight[i] = stage(i)

        advance(stage_one)
        do_output(0)
        do_output(1)
        do_gm_halo()
        advance(stage_two)
        do_grad_clip(0)
        advance(stage_z)
        do_grad_clip(1)
        done = []
        for i in range(len(CHUNKS)):
            finish(flight[i])
            done.append(final(i))
        place(gs_out, jnp.concatenate(done[:2], axis=0), SPATIAL_ROWS)
        place(gt_out, done[2], TEMPORAL_ROWS)

    for c in (clip_up, clip_down, cot_copy, mid_copy, gm_up, gm_down):
        wait_send(c)
    for c in stores:
        c.wait()


def shards(sizes, clip, cot, sw, tw):
    tm_count, h_count = sizes
    frames, rows, cols, ch = clip.shape
    inside = sizes == (4, 8) and ch == 256 and frames == 2
    wide = (frames, rows + 2, cols, 3 * ch)
    edge = (2, frames, cols, ch)
    vmem = pl.BlockSpec(memory_space=pltpu.VMEM)
    scratch = [pltpu.VMEM(x.shape, x.dtype) for x in (clip, cot, sw, tw, clip, clip)]
    scratch += [
        pltpu.SemaphoreType.DMA((4,)),
        pltpu.SemaphoreType.DMA((2 * frames,)),
        pltpu.VMEM(edge, BF16),
        pltpu.VMEM(clip.shape, BF16),
        pltpu.VMEM(clip.shape, BF16),
        pltpu.VMEM(clip.shape, BF16),
        pltpu.VMEM(clip.shape, BF16),
        pltpu.VMEM(edge, BF16),
        pltpu.VMEM(wide, BF16),
        pltpu.VMEM(wide, BF16),
        pltpu.VMEM((3, ch, frames * rows * cols), BF16),
        pltpu.VMEM((9 * ch, ch), F32),
        pltpu.VMEM((3 * ch, ch), F32),
        pltpu.SemaphoreType.DMA((6,)),
        pltpu.SemaphoreType.DMA((6,)),
    ]
    gs_shape, gt_shape = (9 * ch, ch), (3 * ch, ch)
    if inside:
        gs_shape, gt_shape = (2 * SPATIAL_ROWS, LANES), (2 * TEMPORAL_ROWS, LANES)
        for _, _, a, b in CHUNKS:
            n = a + b
            scratch += [pltpu.VMEM((16, n, LANES), BF16)] * 2
            scratch += [pltpu.VMEM((16, n, LANES), F32)]
            scratch += [pltpu.VMEM((8, a, LANES), BF16)] * 2
            scratch += [pltpu.VMEM((8, b, LANES), BF16)] * 2
            scratch += [pltpu.VMEM((4, a, LANES), BF16)] * 2
            scratch += [pltpu.VMEM((4, b, LANES), BF16)] * 2
        for _, _, a, b in CHUNKS:
            n = a + b
            scratch += [
                pltpu.VMEM((4, n, LANES), F32),
                pltpu.VMEM((4, n, LANES), BF16),
                pltpu.VMEM((3, n, LANES), BF16),
            ]
        scratch += [pltpu.SemaphoreType.DMA((8 * len(CHUNKS),))] * 2
    out, gclip, gs, gt = pl.pallas_call(
        functools.partial(body, sizes, inside),
        out_shape=(
            jax.ShapeDtypeStruct(clip.shape, BF16),
            jax.ShapeDtypeStruct(clip.shape, BF16),
            jax.ShapeDtypeStruct(gs_shape, F32),
            jax.ShapeDtypeStruct(gt_shape, F32),
        ),
        in_specs=[pl.BlockSpec(memory_space=pltpu.HBM)] * 4,
        out_specs=(pl.BlockSpec(memory_space=pltpu.HBM),) * 2 + (vmem,) * 2,
        scratch_shapes=scratch,
        compiler_params=pltpu.CompilerParams(
            collective_id=0, has_side_effects=True, vmem_limit_bytes=125 * 1024 * 1024 // 2
        ),
        name="section",
    )(clip, cot, sw, tw)
    gs, gt = gs.reshape(-1), gt.reshape(-1)
    if not inside:
        gs, gt = (
            lax.psum_scatter(gs, ("tm", "height"), scatter_dimension=0, tiled=True),
            lax.psum_scatter(gt, ("tm", "height"), scatter_dimension=0, tiled=True),
        )
    return out, gclip, gs, gt


def solution(mesh):
    sizes = (mesh.shape["tm"], mesh.shape["height"])
    return jax.shard_map(
        functools.partial(shards, sizes),
        mesh=mesh,
        in_specs=(P("tm", "height", None, None), P("tm", "height", None, None), P(), P()),
        out_specs=(
            P("tm", "height", None, None),
            P("tm", "height", None, None),
            P(("tm", "height")),
            P(("tm", "height")),
        ),
        check_vma=False,
    )
```

```python
import functools
import math

import jax
import jax.numpy as jnp
from jax import lax
from jax.experimental import pallas as pl
from jax.experimental.pallas import tpu as pltpu
from jax.sharding import PartitionSpec as P

EPSILON = 1e-06
MESH = pl.DeviceIdType.MESH
F32 = jnp.float32
BF16 = jnp.bfloat16
NN = (((1,), (0,)), ((), ()))
NT = (((1,), (1,)), ((), ()))
TN = (((0,), (0,)), ((), ()))

SPATIAL_ROWS = 72
TEMPORAL_ROWS = 24
LANES = 128
CHUNKS = (("spatial", 0, 32, 32), ("spatial", 64, 32, 48), ("temporal", 0, 32, 16))


def dot(left, right, dims=NN):
    return lax.dot_general(left, right, dims, preferred_element_type=F32)


def flat(block):
    return block.reshape(-1, block.shape[-1])


def activate(values):
    scale_inv = lax.rsqrt(jnp.mean(values * values, axis=-1, keepdims=True) + EPSILON)
    normed = values * scale_inv
    return normed / (1.0 + jnp.exp(-normed))


def columns(block):
    wide = block.astype(F32)
    zero = jnp.zeros(wide.shape[:-2] + (1,) + wide.shape[-1:], F32)
    axis = wide.ndim - 2
    count = wide.shape[axis]
    before = jnp.concatenate([zero, lax.slice_in_dim(wide, 0, count - 1, axis=axis)], axis=axis)
    after = jnp.concatenate([lax.slice_in_dim(wide, 1, count, axis=axis), zero], axis=axis)
    return before.astype(BF16), block.astype(BF16), after.astype(BF16)


def body(
    sizes, reduce_inside, clip_hbm, cot_hbm, sw_hbm, tw_hbm, out_hbm, gclip_hbm, gs_out, gt_out,
    clip, sw, tw, out, gclip, in_sem, out_sem,
    clip_halo, cot_ext, mid_ext, mid_t, gm, gm_halo, act3, gm3, act_t, grad_act, gs, gt, hsend, hrecv, *rest
):
    tm_count, h_count = sizes
    frames, rows, cols, ch = clip.shape
    block = (frames, rows, cols, ch)
    tm = lax.axis_index("tm")
    hh = lax.axis_index("height")
    cells = rows * cols

    cot, cot_next = cot_ext.at[pl.ds(0, frames)], cot_ext.at[pl.ds(frames, frames)]
    mid_prev, mid = mid_ext.at[pl.ds(0, frames)], mid_ext.at[pl.ds(frames, frames)]

    loads = [
        pltpu.make_async_copy(src, dst, in_sem.at[i])
        for i, (src, dst) in enumerate(
            ((clip_hbm, clip), (cot_hbm, cot), (sw_hbm, sw), (tw_hbm, tw))
        )
    ]
    for load in loads:
        load.start()

    up, down = {"height": hh - 1}, {"height": hh + 1}
    before, after = {"tm": tm - 1}, {"tm": tm + 1}
    has_up, has_down = hh > 0, hh < h_count - 1
    has_before, has_after = tm > 0, tm < tm_count - 1

    barrier = pltpu.get_barrier_semaphore()

    def greet(where, who):
        @pl.when(where)
        def _():
            pl.semaphore_signal(barrier, inc=1, device_id=who, device_id_type=MESH)

    sides = ((has_up, up), (has_down, down), (has_before, before), (has_after, after))
    for where, who in sides:
        greet(where, who)
    if reduce_inside:
        core, xx, yy, zz = lax.rem(tm, 2), tm // 2, lax.rem(hh, 2), hh // 2
        by_core = {"tm": xx * 2 + 1 - core}
        by_x = {"tm": (1 - xx) * 2 + core}
        by_y = {"height": zz * 2 + 1 - yy}
        by_z = [{"height": lax.rem(zz + off, 4) * 2 + yy} for off in (1, 2, 3)]
        for who in [by_core, by_x, by_y] + by_z:
            pl.semaphore_signal(barrier, inc=1, device_id=who, device_id_type=MESH)

    greeted = 6 if reduce_inside else 0
    for where, who in sides:
        greeted = greeted + where.astype(jnp.int32)
    pl.semaphore_wait(barrier, greeted)

    def copy(src, dst, slot, who):
        return pltpu.make_async_remote_copy(
            src_ref=src, dst_ref=dst, send_sem=hsend.at[slot], recv_sem=hrecv.at[slot],
            device_id=who, device_id_type=MESH,
        )

    def exchange(slot, src_first, src_last, dst, send_up, send_down):
        return (
            (copy(src_first, dst.at[1], slot, up), has_up, has_down),
            (copy(src_last, dst.at[0], slot + 1, down), has_down, has_up),
        )

    def start(c):
        @pl.when(c[1])
        def _():
            c[0].start()

    def wait_recv(c, target):
        @pl.when(c[2])
        def _():
            c[0].wait_recv()

        @pl.when(jnp.logical_not(c[2]))
        def _():
            target[...] = jnp.zeros(target.shape, target.dtype)

    def wait_send(c):
        @pl.when(c[1])
        def _():
            c[0].wait_send()

    cot_copy = (copy(cot_hbm, cot_next, 0, before), has_before, has_after)
    clip_up, clip_down = exchange(1, clip_hbm.at[:, 0], clip_hbm.at[:, rows - 1], clip_halo, up, down)
    start(clip_up)
    start(clip_down)
    start(cot_copy)

    loads[0].wait()

    def put_act(f, row, values):
        act = activate(values.astype(F32))
        for q, part in enumerate(columns(act)):
            act3[f, row, :, pl.ds(q * ch, ch)] = part

    for f in range(frames):
        for row in range(rows):
            put_act(f, row + 1, clip[f, row])
    wait_recv(clip_up, clip_halo.at[1])
    wait_recv(clip_down, clip_halo.at[0])
    for f in range(frames):
        put_act(f, 0, clip_halo[0, f])
        put_act(f, rows + 1, clip_halo[1, f])

    loads[2].wait()
    total = None
    for r in range(3):
        term = dot(flat(act3[:, r : r + rows]), flat(sw[r]))
        total = term if total is None else total + term
    mid_ext[frames:] = total.astype(BF16).reshape(block)
    mid_copy = (copy(mid, mid_prev, 3, after), has_after, has_before)
    start(mid_copy)

    for r in range(3):
        for f in range(frames):
            act_t[pl.ds(r * ch, ch), pl.ds(f * cells, cells)] = flat(
                act3[f, r : r + rows, :, pl.ds(ch, ch)]
            ).T

    loads[1].wait()
    loads[3].wait()
    wait_recv(cot_copy, cot_next)

    def put_gm(f, row, values):
        shifts = columns(values)
        for q in range(3):
            gm3[f, row, :, pl.ds(q * ch, ch)] = shifts[2 - q]

    total = None
    for k in range(3):
        term = dot(flat(cot_ext[k : k + frames]), tw[k], NT)
        total = term if total is None else total + term
    value = total.astype(BF16).reshape(block)
    gm[...] = value
    gm_up, gm_down = exchange(4, gm.at[:, 0], gm.at[:, rows - 1], gm_halo, up, down)
    start(gm_up)
    start(gm_down)
    for f in range(frames):
        for row in range(rows):
            put_gm(f, row + 1, value[f, row])

    for q in range(3):
        total = dot(act_t[...], flat(gm3[:, 1 : 1 + rows, :, pl.ds(q * ch, ch)]))
        for r in range(3):
            gs[pl.ds((r * 3 + q) * ch, ch), :] = total[r * ch : (r + 1) * ch]

    def turn_mid(t):
        mid_t[:, pl.ds(t * cells, cells)] = flat(mid_ext[t]).T

    def do_temporal():
        for t in range(frames, 2 * frames):
            turn_mid(t)
        wait_recv(mid_copy, mid_prev)
        for t in range(frames):
            turn_mid(t)
        left = jnp.concatenate(
            [mid_t[:, pl.ds((frames - k) * cells, frames * cells)] for k in range(3)], axis=0
        )
        gt[...] = dot(left, flat(cot_ext[:frames]))

    stores = []

    def store(src, dst, slot):
        c = pltpu.make_async_copy(src, dst, out_sem.at[slot])
        c.start()
        stores.append(c)

    def do_output():
        total = flat(clip[...]).astype(F32)
        for k in range(3):
            total = total + dot(flat(mid_ext[frames - k : 2 * frames - k]), tw[k])
        out[...] = total.astype(BF16).reshape(block)
        store(out, out_hbm, 0)

    def do_gm_halo():
        wait_recv(gm_up, gm_halo.at[1])
        wait_recv(gm_down, gm_halo.at[0])
        for f in range(frames):
            put_gm(f, 0, gm_halo[0, f])
            put_gm(f, rows + 1, gm_halo[1, f])

    def do_grad_act():
        total = None
        for r in range(3):
            for q in range(3):
                left = flat(gm3[:, 2 - r : 2 - r + rows, :, pl.ds(q * ch, ch)])
                term = dot(left, sw[r, q], NT)
                total = term if total is None else total + term
        grad_act[...] = total

    def do_grad_clip():
        for f in range(frames):
            values = flat(clip[f]).astype(F32)
            scale_inv = lax.rsqrt(jnp.mean(values * values, axis=-1, keepdims=True) + EPSILON)
            normed = values * scale_inv
            gate = 1.0 / (1.0 + jnp.exp(-normed))
            inner = grad_act[pl.ds(f * cells, cells), :] * (gate * (1.0 + normed * (1.0 - gate)))
            slope = scale_inv * (
                inner - normed * jnp.mean(inner * normed, axis=-1, keepdims=True)
            )
            total = flat(cot_ext[f]).astype(F32) + slope
            gclip[f] = total.astype(BF16).reshape(rows, cols, ch)
        store(gclip, gclip_hbm, 1)

    scale = 1.0 / math.sqrt(frames * tm_count * rows * h_count * cols)

    if not reduce_inside:
        do_temporal()
        do_output()
        do_gm_halo()
        do_grad_act()
        do_grad_clip()
        gs_out[...] = gs[...] * scale
        gt_out[...] = gt[...] * scale
    else:
        rsend, rrecv = rest[-2:]
        bufs = [rest[11 * i : 11 * i + 11] for i in range(len(CHUNKS))]

        def rcopy(src, dst, slot, who):
            return pltpu.make_async_remote_copy(
                src_ref=src, dst_ref=dst, send_sem=rsend.at[slot], recv_sem=rrecv.at[slot],
                device_id=who, device_id_type=MESH,
            )

        def piece(chunk, d):
            kind, first, a, b = chunk
            ref, count = (gs, SPATIAL_ROWS) if kind == "spatial" else (gt, TEMPORAL_ROWS)
            block = ref[pl.ds(pl.multiple_of(d * count, 8), count), :]
            both = jnp.concatenate([block[:, :LANES], block[:, LANES:]], axis=0)
            return both[first : first + a + b]

        def each(count):
            def run(step):
                def four(j, carry):
                    for i in range(4):
                        step(j * 4 + i)
                    return carry

                lax.fori_loop(0, count // 4, four, 0)

            return run

        def owner(j, which):
            return ((j // 8) * 2 + which) * 8 + lax.rem(j, 8)

        def stage_core(i):
            send0, recv0 = bufs[i][:2]

            @each(16)
            def _(j):
                send0[j] = piece(CHUNKS[i], owner(j, 1 - core)).astype(BF16)

            c = rcopy(send0, recv0, 8 * i, by_core)
            c.start()
            return [c]

        def stage_one(i):
            a = CHUNKS[i][2]
            send0, recv0, part, send_a, recv_a, send_b, recv_b = bufs[i][:7]

            @each(16)
            def _(j):
                part[j] = piece(CHUNKS[i], owner(j, core)) + recv0[j].astype(F32)

            @each(8)
            def _(j):
                send_a[j] = part[(1 - xx) * 8 + j, :a].astype(BF16)
                send_b[j] = part[j * 2 + 1 - yy, a:].astype(BF16)

            cs = [
                rcopy(send_a, recv_a, 8 * i + 1, by_x),
                rcopy(send_b, recv_b, 8 * i + 2, by_y),
            ]
            for c in cs:
                c.start()
            return cs

        def stage_two(i):
            a = CHUNKS[i][2]
            part, _, recv_a, _, recv_b, send_a2, recv_a2, send_b2, recv_b2 = bufs[i][2:11]

            @each(4)
            def _(j):
                away = j * 2 + 1 - yy
                send_a2[j] = (part[xx * 8 + away, :a] + recv_a[away].astype(F32)).astype(BF16)
                far = (1 - xx) * 4 + j
                send_b2[j] = (part[far * 2 + yy, a:] + recv_b[far].astype(F32)).astype(BF16)

            cs = [
                rcopy(send_a2, recv_a2, 8 * i + 3, by_y),
                rcopy(send_b2, recv_b2, 8 * i + 4, by_x),
            ]
            for c in cs:
                c.start()
            return cs

        z_bufs = rest[11 * len(CHUNKS) : -2]

        def stage_z(i):
            a = CHUNKS[i][2]
            part, _, recv_a, _, recv_b, _, recv_a2, _, recv_b2 = bufs[i][2:11]
            total_z, send_z, recv_z = z_bufs[3 * i : 3 * i + 3]

            @each(4)
            def _(j):
                near = j * 2 + yy
                first = part[xx * 8 + near, :a] + recv_a[near].astype(F32) + recv_a2[j].astype(F32)
                last = (
                    part[xx * 8 + near, a:] + recv_b[xx * 4 + j].astype(F32) + recv_b2[j].astype(F32)
                )
                value = jnp.concatenate([first, last], axis=0)
                total_z[j] = value
                send_z[j] = value.astype(BF16)

            cs = [
                rcopy(
                    send_z.at[lax.rem(zz + off, 4)], recv_z.at[off - 1], 8 * i + 4 + off, by_z[off - 1]
                )
                for off in (1, 2, 3)
            ]
            for c in cs:
                c.start()
            return cs

        def final(i):
            total_z, _, recv_z = z_bufs[3 * i : 3 * i + 3]
            value = total_z[zz]
            for off in range(3):
                value = value + recv_z[off].astype(F32)
            return value * scale

        def finish(copies):
            for c in copies:
                c.wait()

        def place(ref, value, count):
            ref[pl.ds(0, count, stride=2), :] = value[:count]
            ref[pl.ds(1, count, stride=2), :] = value[count:]

        spatial = (0, 1)
        flight = {i: stage_core(i) for i in spatial}
        do_temporal()
        flight[2] = stage_core(2)

        def advance(stage):
            for i in range(len(CHUNKS)):
                finish(flight[i])
                flight[i] = stage(i)

        advance(stage_one)
        do_output()
        do_gm_halo()
        advance(stage_two)
        do_grad_act()
        advance(stage_z)
        do_grad_clip()
        done = []
        for i in range(len(CHUNKS)):
            finish(flight[i])
            done.append(final(i))
        place(gs_out, jnp.concatenate(done[:2], axis=0), SPATIAL_ROWS)
        place(gt_out, done[2], TEMPORAL_ROWS)

    for c in (clip_up, clip_down, cot_copy, mid_copy, gm_up, gm_down):
        wait_send(c)
    for c in stores:
        c.wait()


def hand_on(*refs):
    count = len(refs) // 2
    copies = [
        pltpu.make_async_copy(refs[i], refs[count + i], refs[-1].at[i]) for i in range(count)
    ]
    for c in copies:
        c.start()
    for c in copies:
        c.wait()


def handed_on(*arrays):
    place = pl.BlockSpec(memory_space=pltpu.HBM)
    return pl.pallas_call(
        hand_on,
        out_shape=tuple(jax.ShapeDtypeStruct(x.shape, x.dtype) for x in arrays),
        in_specs=[place] * len(arrays),
        out_specs=(place,) * len(arrays),
        scratch_shapes=[pltpu.SemaphoreType.DMA((len(arrays),))],
        compiler_params=pltpu.CompilerParams(vmem_limit_bytes=125 * 1024 * 1024 // 2),
        name="hand_on",
    )(*arrays)


def shards(sizes, clip, cot, sw, tw):
    tm_count, h_count = sizes
    frames, rows, cols, ch = clip.shape
    inside = sizes == (4, 8) and ch == 256 and frames == 2
    wide = (frames, rows + 2, cols, 3 * ch)
    edge = (2, frames, cols, ch)
    vmem = pl.BlockSpec(memory_space=pltpu.VMEM)
    scratch = [pltpu.VMEM(x.shape, x.dtype) for x in (clip, sw, tw, clip, clip)]
    scratch += [
        pltpu.SemaphoreType.DMA((4,)),
        pltpu.SemaphoreType.DMA((2,)),
        pltpu.VMEM(edge, BF16),
        pltpu.VMEM((2 * frames, rows, cols, ch), BF16),
        pltpu.VMEM((2 * frames, rows, cols, ch), BF16),
        pltpu.VMEM((ch, 2 * frames * rows * cols), BF16),
        pltpu.VMEM(clip.shape, BF16),
        pltpu.VMEM(edge, BF16),
        pltpu.VMEM(wide, BF16),
        pltpu.VMEM(wide, BF16),
        pltpu.VMEM((3 * ch, frames * rows * cols), BF16),
        pltpu.VMEM((frames * rows * cols, ch), F32),
        pltpu.VMEM((9 * ch, ch), F32),
        pltpu.VMEM((3 * ch, ch), F32),
        pltpu.SemaphoreType.DMA((6,)),
        pltpu.SemaphoreType.DMA((6,)),
    ]
    gs_shape, gt_shape = (9 * ch, ch), (3 * ch, ch)
    if inside:
        gs_shape, gt_shape = (2 * SPATIAL_ROWS, LANES), (2 * TEMPORAL_ROWS, LANES)
        for _, _, a, b in CHUNKS:
            n = a + b
            scratch += [pltpu.VMEM((16, n, LANES), BF16)] * 2
            scratch += [pltpu.VMEM((16, n, LANES), F32)]
            scratch += [pltpu.VMEM((8, a, LANES), BF16)] * 2
            scratch += [pltpu.VMEM((8, b, LANES), BF16)] * 2
            scratch += [pltpu.VMEM((4, a, LANES), BF16)] * 2
            scratch += [pltpu.VMEM((4, b, LANES), BF16)] * 2
        for _, _, a, b in CHUNKS:
            n = a + b
            scratch += [
                pltpu.VMEM((4, n, LANES), F32),
                pltpu.VMEM((4, n, LANES), BF16),
                pltpu.VMEM((3, n, LANES), BF16),
            ]
        scratch += [pltpu.SemaphoreType.DMA((8 * len(CHUNKS),))] * 2
    out, gclip, gs, gt = pl.pallas_call(
        functools.partial(body, sizes, inside),
        out_shape=(
            jax.ShapeDtypeStruct(clip.shape, BF16),
            jax.ShapeDtypeStruct(clip.shape, BF16),
            jax.ShapeDtypeStruct(gs_shape, F32),
            jax.ShapeDtypeStruct(gt_shape, F32),
        ),
        in_specs=[pl.BlockSpec(memory_space=pltpu.HBM)] * 4,
        out_specs=(pl.BlockSpec(memory_space=pltpu.HBM),) * 2 + (vmem,) * 2,
        scratch_shapes=scratch,
        compiler_params=pltpu.CompilerParams(
            collective_id=0, has_side_effects=True, vmem_limit_bytes=125 * 1024 * 1024 // 2
        ),
        name="section",
    )(clip, cot, sw, tw)
    if inside:
        out, gclip, gs, gt = handed_on(out, gclip, gs, gt)
    gs, gt = gs.reshape(-1), gt.reshape(-1)
    if not inside:
        gs, gt = (
            lax.psum_scatter(gs, ("tm", "height"), scatter_dimension=0, tiled=True),
            lax.psum_scatter(gt, ("tm", "height"), scatter_dimension=0, tiled=True),
        )
    return out, gclip, gs, gt


def solution(mesh):
    sizes = (mesh.shape["tm"], mesh.shape["height"])
    return jax.shard_map(
        functools.partial(shards, sizes),
        mesh=mesh,
        in_specs=(P("tm", "height", None, None), P("tm", "height", None, None), P(), P()),
        out_specs=(
            P("tm", "height", None, None),
            P("tm", "height", None, None),
            P(("tm", "height")),
            P(("tm", "height")),
        ),
        check_vma=False,
    )
```

```python
import functools
import math

import jax
import jax.numpy as jnp
from jax import lax
from jax.experimental import pallas as pl
from jax.experimental.pallas import tpu as pltpu
from jax.sharding import PartitionSpec as P

EPSILON = 1e-06
MESH = pl.DeviceIdType.MESH
F32 = jnp.float32
BF16 = jnp.bfloat16
NN = (((1,), (0,)), ((), ()))
NT = (((1,), (1,)), ((), ()))
TN = (((0,), (0,)), ((), ()))

SPATIAL_ROWS = 72
TEMPORAL_ROWS = 24
LANES = 128
CHUNKS = (("spatial", 0, 32, 32), ("spatial", 64, 32, 48), ("temporal", 0, 32, 16))


def dot(left, right, dims=NN):
    return lax.dot_general(left, right, dims, preferred_element_type=F32)


def flat(block):
    return block.reshape(-1, block.shape[-1])


def activate(values):
    scale_inv = lax.rsqrt(jnp.mean(values * values, axis=-1, keepdims=True) + EPSILON)
    normed = values * scale_inv
    return normed / (1.0 + jnp.exp(-normed))


def columns(block):
    wide = block.astype(F32)
    zero = jnp.zeros(wide.shape[:-2] + (1,) + wide.shape[-1:], F32)
    axis = wide.ndim - 2
    count = wide.shape[axis]
    before = jnp.concatenate([zero, lax.slice_in_dim(wide, 0, count - 1, axis=axis)], axis=axis)
    after = jnp.concatenate([lax.slice_in_dim(wide, 1, count, axis=axis), zero], axis=axis)
    return before.astype(BF16), block.astype(BF16), after.astype(BF16)


def body(
    sizes, reduce_inside, clip_hbm, cot_hbm, sw_hbm, tw_hbm, out, gclip, gs_out, gt_out,
    clip, sw, tw, in_sem,
    clip_halo, cot_ext, mid_ext, mid_t, gm, gm_halo, act3, gm3, act_t, grad_act, gs, gt, hsend, hrecv, *rest
):
    tm_count, h_count = sizes
    frames, rows, cols, ch = clip.shape
    block = (frames, rows, cols, ch)
    tm = lax.axis_index("tm")
    hh = lax.axis_index("height")
    cells = rows * cols

    cot, cot_next = cot_ext.at[pl.ds(0, frames)], cot_ext.at[pl.ds(frames, frames)]
    mid_prev, mid = mid_ext.at[pl.ds(0, frames)], mid_ext.at[pl.ds(frames, frames)]

    loads = [
        pltpu.make_async_copy(src, dst, in_sem.at[i])
        for i, (src, dst) in enumerate(
            ((clip_hbm, clip), (cot_hbm, cot), (sw_hbm, sw), (tw_hbm, tw))
        )
    ]
    for load in loads:
        load.start()

    up, down = {"height": hh - 1}, {"height": hh + 1}
    before, after = {"tm": tm - 1}, {"tm": tm + 1}
    has_up, has_down = hh > 0, hh < h_count - 1
    has_before, has_after = tm > 0, tm < tm_count - 1

    barrier = pltpu.get_barrier_semaphore()

    def greet(where, who):
        @pl.when(where)
        def _():
            pl.semaphore_signal(barrier, inc=1, device_id=who, device_id_type=MESH)

    sides = ((has_up, up), (has_down, down), (has_before, before), (has_after, after))
    for where, who in sides:
        greet(where, who)
    if reduce_inside:
        core, xx, yy, zz = lax.rem(tm, 2), tm // 2, lax.rem(hh, 2), hh // 2
        by_core = {"tm": xx * 2 + 1 - core}
        by_x = {"tm": (1 - xx) * 2 + core}
        by_y = {"height": zz * 2 + 1 - yy}
        by_z = [{"height": lax.rem(zz + off, 4) * 2 + yy} for off in (1, 2, 3)]
        for who in [by_core, by_x, by_y] + by_z:
            pl.semaphore_signal(barrier, inc=1, device_id=who, device_id_type=MESH)

    greeted = 6 if reduce_inside else 0
    for where, who in sides:
        greeted = greeted + where.astype(jnp.int32)
    pl.semaphore_wait(barrier, greeted)

    def copy(src, dst, slot, who):
        return pltpu.make_async_remote_copy(
            src_ref=src, dst_ref=dst, send_sem=hsend.at[slot], recv_sem=hrecv.at[slot],
            device_id=who, device_id_type=MESH,
        )

    def exchange(slot, src_first, src_last, dst, send_up, send_down):
        return (
            (copy(src_first, dst.at[1], slot, up), has_up, has_down),
            (copy(src_last, dst.at[0], slot + 1, down), has_down, has_up),
        )

    def start(c):
        @pl.when(c[1])
        def _():
            c[0].start()

    def wait_recv(c, target):
        @pl.when(c[2])
        def _():
            c[0].wait_recv()

        @pl.when(jnp.logical_not(c[2]))
        def _():
            target[...] = jnp.zeros(target.shape, target.dtype)

    def wait_send(c):
        @pl.when(c[1])
        def _():
            c[0].wait_send()

    cot_copy = (copy(cot_hbm, cot_next, 0, before), has_before, has_after)
    clip_up, clip_down = exchange(1, clip_hbm.at[:, 0], clip_hbm.at[:, rows - 1], clip_halo, up, down)
    start(clip_up)
    start(clip_down)
    start(cot_copy)

    loads[0].wait()

    def put_act(f, row, values):
        act = activate(values.astype(F32))
        for q, part in enumerate(columns(act)):
            act3[f, row, :, pl.ds(q * ch, ch)] = part

    for f in range(frames):
        for row in range(rows):
            put_act(f, row + 1, clip[f, row])
    wait_recv(clip_up, clip_halo.at[1])
    wait_recv(clip_down, clip_halo.at[0])
    for f in range(frames):
        put_act(f, 0, clip_halo[0, f])
        put_act(f, rows + 1, clip_halo[1, f])

    loads[2].wait()
    total = None
    for r in range(3):
        term = dot(flat(act3[:, r : r + rows]), flat(sw[r]))
        total = term if total is None else total + term
    mid_ext[frames:] = total.astype(BF16).reshape(block)
    mid_copy = (copy(mid, mid_prev, 3, after), has_after, has_before)
    start(mid_copy)

    for r in range(3):
        for f in range(frames):
            act_t[pl.ds(r * ch, ch), pl.ds(f * cells, cells)] = flat(
                act3[f, r : r + rows, :, pl.ds(ch, ch)]
            ).T

    loads[1].wait()
    loads[3].wait()
    wait_recv(cot_copy, cot_next)

    def put_gm(f, row, values):
        shifts = columns(values)
        for q in range(3):
            gm3[f, row, :, pl.ds(q * ch, ch)] = shifts[2 - q]

    total = None
    for k in range(3):
        term = dot(flat(cot_ext[k : k + frames]), tw[k], NT)
        total = term if total is None else total + term
    value = total.astype(BF16).reshape(block)
    gm[...] = value
    gm_up, gm_down = exchange(4, gm.at[:, 0], gm.at[:, rows - 1], gm_halo, up, down)
    start(gm_up)
    start(gm_down)
    for f in range(frames):
        for row in range(rows):
            put_gm(f, row + 1, value[f, row])

    for q in range(3):
        total = dot(act_t[...], flat(gm3[:, 1 : 1 + rows, :, pl.ds(q * ch, ch)]))
        for r in range(3):
            gs[pl.ds((r * 3 + q) * ch, ch), :] = total[r * ch : (r + 1) * ch]

    def turn_mid(t):
        mid_t[:, pl.ds(t * cells, cells)] = flat(mid_ext[t]).T

    def do_temporal():
        for t in range(frames, 2 * frames):
            turn_mid(t)
        wait_recv(mid_copy, mid_prev)
        for t in range(frames):
            turn_mid(t)
        left = jnp.concatenate(
            [mid_t[:, pl.ds((frames - k) * cells, frames * cells)] for k in range(3)], axis=0
        )
        gt[...] = dot(left, flat(cot_ext[:frames]))

    def do_output():
        total = flat(clip[...]).astype(F32)
        for k in range(3):
            total = total + dot(flat(mid_ext[frames - k : 2 * frames - k]), tw[k])
        out[...] = total.astype(BF16).reshape(block)

    def do_gm_halo():
        wait_recv(gm_up, gm_halo.at[1])
        wait_recv(gm_down, gm_halo.at[0])
        for f in range(frames):
            put_gm(f, 0, gm_halo[0, f])
            put_gm(f, rows + 1, gm_halo[1, f])

    def do_grad_act(r):
        total = None
        for q in range(3):
            left = flat(gm3[:, 2 - r : 2 - r + rows, :, pl.ds(q * ch, ch)])
            term = dot(left, sw[r, q], NT)
            total = term if total is None else total + term
        if r == 0:
            grad_act[...] = total
        else:
            grad_act[...] += total

    def do_grad_clip():
        for f in range(frames):
            values = flat(clip[f]).astype(F32)
            scale_inv = lax.rsqrt(jnp.mean(values * values, axis=-1, keepdims=True) + EPSILON)
            normed = values * scale_inv
            gate = 1.0 / (1.0 + jnp.exp(-normed))
            inner = grad_act[pl.ds(f * cells, cells), :] * (gate * (1.0 + normed * (1.0 - gate)))
            slope = scale_inv * (
                inner - normed * jnp.mean(inner * normed, axis=-1, keepdims=True)
            )
            total = flat(cot_ext[f]).astype(F32) + slope
            gclip[f] = total.astype(BF16).reshape(rows, cols, ch)

    scale = 1.0 / math.sqrt(frames * tm_count * rows * h_count * cols)

    if not reduce_inside:
        do_temporal()
        do_output()
        do_gm_halo()
        for r in range(3):
            do_grad_act(r)
        do_grad_clip()
        gs_out[...] = gs[...] * scale
        gt_out[...] = gt[...] * scale
    else:
        rsend, rrecv = rest[-2:]
        bufs = [rest[11 * i : 11 * i + 11] for i in range(len(CHUNKS))]

        def rcopy(src, dst, slot, who):
            return pltpu.make_async_remote_copy(
                src_ref=src, dst_ref=dst, send_sem=rsend.at[slot], recv_sem=rrecv.at[slot],
                device_id=who, device_id_type=MESH,
            )

        def piece(chunk, d):
            kind, first, a, b = chunk
            ref, count = (gs, SPATIAL_ROWS) if kind == "spatial" else (gt, TEMPORAL_ROWS)
            block = ref[pl.ds(pl.multiple_of(d * count, 8), count), :]
            both = jnp.concatenate([block[:, :LANES], block[:, LANES:]], axis=0)
            return both[first : first + a + b]

        def each(count):
            def run(step):
                def four(j, carry):
                    for i in range(4):
                        step(j * 4 + i)
                    return carry

                lax.fori_loop(0, count // 4, four, 0)

            return run

        def owner(j, which):
            return ((j // 8) * 2 + which) * 8 + lax.rem(j, 8)

        def stage_core(i):
            send0, recv0 = bufs[i][:2]

            @each(16)
            def _(j):
                send0[j] = piece(CHUNKS[i], owner(j, 1 - core)).astype(BF16)

            c = rcopy(send0, recv0, 8 * i, by_core)
            c.start()
            return [c]

        def stage_one(i):
            a = CHUNKS[i][2]
            send0, recv0, part, send_a, recv_a, send_b, recv_b = bufs[i][:7]

            @each(16)
            def _(j):
                part[j] = piece(CHUNKS[i], owner(j, core)) + recv0[j].astype(F32)

            @each(8)
            def _(j):
                send_a[j] = part[(1 - xx) * 8 + j, :a].astype(BF16)
                send_b[j] = part[j * 2 + 1 - yy, a:].astype(BF16)

            cs = [
                rcopy(send_a, recv_a, 8 * i + 1, by_x),
                rcopy(send_b, recv_b, 8 * i + 2, by_y),
            ]
            for c in cs:
                c.start()
            return cs

        def stage_two(i):
            a = CHUNKS[i][2]
            part, _, recv_a, _, recv_b, send_a2, recv_a2, send_b2, recv_b2 = bufs[i][2:11]

            @each(4)
            def _(j):
                away = j * 2 + 1 - yy
                send_a2[j] = (part[xx * 8 + away, :a] + recv_a[away].astype(F32)).astype(BF16)
                far = (1 - xx) * 4 + j
                send_b2[j] = (part[far * 2 + yy, a:] + recv_b[far].astype(F32)).astype(BF16)

            cs = [
                rcopy(send_a2, recv_a2, 8 * i + 3, by_y),
                rcopy(send_b2, recv_b2, 8 * i + 4, by_x),
            ]
            for c in cs:
                c.start()
            return cs

        z_bufs = rest[11 * len(CHUNKS) : -2]

        def stage_z(i):
            a = CHUNKS[i][2]
            part, _, recv_a, _, recv_b, _, recv_a2, _, recv_b2 = bufs[i][2:11]
            total_z, send_z, recv_z = z_bufs[3 * i : 3 * i + 3]

            @each(4)
            def _(j):
                near = j * 2 + yy
                first = part[xx * 8 + near, :a] + recv_a[near].astype(F32) + recv_a2[j].astype(F32)
                last = (
                    part[xx * 8 + near, a:] + recv_b[xx * 4 + j].astype(F32) + recv_b2[j].astype(F32)
                )
                value = jnp.concatenate([first, last], axis=0)
                total_z[j] = value
                send_z[j] = value.astype(BF16)

            cs = [
                rcopy(
                    send_z.at[lax.rem(zz + off, 4)], recv_z.at[off - 1], 8 * i + 4 + off, by_z[off - 1]
                )
                for off in (1, 2, 3)
            ]
            for c in cs:
                c.start()
            return cs

        def final(i):
            total_z, _, recv_z = z_bufs[3 * i : 3 * i + 3]
            value = total_z[zz]
            for off in range(3):
                value = value + recv_z[off].astype(F32)
            return value * scale

        def finish(copies):
            for c in copies:
                c.wait()

        def place(ref, value, count):
            ref[pl.ds(0, count, stride=2), :] = value[:count]
            ref[pl.ds(1, count, stride=2), :] = value[count:]

        spatial = (0, 1)
        flight = {i: stage_core(i) for i in spatial}
        do_temporal()
        flight[2] = stage_core(2)

        def advance(stage):
            for i in range(len(CHUNKS)):
                finish(flight[i])
                flight[i] = stage(i)

        advance(stage_one)
        do_output()
        do_gm_halo()
        do_grad_act(0)
        advance(stage_two)
        do_grad_act(1)
        advance(stage_z)
        do_grad_act(2)
        do_grad_clip()
        done = []
        for i in range(len(CHUNKS)):
            finish(flight[i])
            done.append(final(i))
        place(gs_out, jnp.concatenate(done[:2], axis=0), SPATIAL_ROWS)
        place(gt_out, done[2], TEMPORAL_ROWS)

    for c in (clip_up, clip_down, cot_copy, mid_copy, gm_up, gm_down):
        wait_send(c)


def hand_on(*refs):
    count = len(refs) // 2
    copies = [
        pltpu.make_async_copy(refs[i], refs[count + i], refs[-1].at[i]) for i in range(count)
    ]
    for c in copies:
        c.start()
    for c in copies:
        c.wait()


def handed_on(*arrays):
    place = pl.BlockSpec(memory_space=pltpu.HBM)
    return pl.pallas_call(
        hand_on,
        out_shape=tuple(jax.ShapeDtypeStruct(x.shape, x.dtype) for x in arrays),
        in_specs=[pl.BlockSpec(memory_space=pltpu.VMEM)] * len(arrays),
        out_specs=(place,) * len(arrays),
        scratch_shapes=[pltpu.SemaphoreType.DMA((len(arrays),))],
        compiler_params=pltpu.CompilerParams(vmem_limit_bytes=4 * 1024 * 1024),
        name="hand_on",
    )(*arrays)


def shards(sizes, clip, cot, sw, tw):
    tm_count, h_count = sizes
    frames, rows, cols, ch = clip.shape
    inside = sizes == (4, 8) and ch == 256 and frames == 2
    wide = (frames, rows + 2, cols, 3 * ch)
    edge = (2, frames, cols, ch)
    vmem = pl.BlockSpec(memory_space=pltpu.VMEM)
    scratch = [pltpu.VMEM(x.shape, x.dtype) for x in (clip, sw, tw)]
    scratch += [
        pltpu.SemaphoreType.DMA((4,)),
        pltpu.VMEM(edge, BF16),
        pltpu.VMEM((2 * frames, rows, cols, ch), BF16),
        pltpu.VMEM((2 * frames, rows, cols, ch), BF16),
        pltpu.VMEM((ch, 2 * frames * rows * cols), BF16),
        pltpu.VMEM(clip.shape, BF16),
        pltpu.VMEM(edge, BF16),
        pltpu.VMEM(wide, BF16),
        pltpu.VMEM(wide, BF16),
        pltpu.VMEM((3 * ch, frames * rows * cols), BF16),
        pltpu.VMEM((frames * rows * cols, ch), F32),
        pltpu.VMEM((9 * ch, ch), F32),
        pltpu.VMEM((3 * ch, ch), F32),
        pltpu.SemaphoreType.DMA((6,)),
        pltpu.SemaphoreType.DMA((6,)),
    ]
    gs_shape, gt_shape = (9 * ch, ch), (3 * ch, ch)
    if inside:
        gs_shape, gt_shape = (2 * SPATIAL_ROWS, LANES), (2 * TEMPORAL_ROWS, LANES)
        for _, _, a, b in CHUNKS:
            n = a + b
            scratch += [pltpu.VMEM((16, n, LANES), BF16)] * 2
            scratch += [pltpu.VMEM((16, n, LANES), F32)]
            scratch += [pltpu.VMEM((8, a, LANES), BF16)] * 2
            scratch += [pltpu.VMEM((8, b, LANES), BF16)] * 2
            scratch += [pltpu.VMEM((4, a, LANES), BF16)] * 2
            scratch += [pltpu.VMEM((4, b, LANES), BF16)] * 2
        for _, _, a, b in CHUNKS:
            n = a + b
            scratch += [
                pltpu.VMEM((4, n, LANES), F32),
                pltpu.VMEM((4, n, LANES), BF16),
                pltpu.VMEM((3, n, LANES), BF16),
            ]
        scratch += [pltpu.SemaphoreType.DMA((8 * len(CHUNKS),))] * 2
    out, gclip, gs, gt = pl.pallas_call(
        functools.partial(body, sizes, inside),
        out_shape=(
            jax.ShapeDtypeStruct(clip.shape, BF16),
            jax.ShapeDtypeStruct(clip.shape, BF16),
            jax.ShapeDtypeStruct(gs_shape, F32),
            jax.ShapeDtypeStruct(gt_shape, F32),
        ),
        in_specs=[pl.BlockSpec(memory_space=pltpu.HBM)] * 4,
        out_specs=(vmem,) * 4,
        scratch_shapes=scratch,
        compiler_params=pltpu.CompilerParams(
            collective_id=0, has_side_effects=True, vmem_limit_bytes=531 * 1024 * 1024 // 10
        ),
        name="section",
    )(clip, cot, sw, tw)
    if inside:
        out, gclip, gs, gt = handed_on(out, gclip, gs, gt)
    gs, gt = gs.reshape(-1), gt.reshape(-1)
    if not inside:
        gs, gt = (
            lax.psum_scatter(gs, ("tm", "height"), scatter_dimension=0, tiled=True),
            lax.psum_scatter(gt, ("tm", "height"), scatter_dimension=0, tiled=True),
        )
    return out, gclip, gs, gt


def solution(mesh):
    sizes = (mesh.shape["tm"], mesh.shape["height"])
    return jax.shard_map(
        functools.partial(shards, sizes),
        mesh=mesh,
        in_specs=(P("tm", "height", None, None), P("tm", "height", None, None), P(), P()),
        out_specs=(
            P("tm", "height", None, None),
            P("tm", "height", None, None),
            P(("tm", "height")),
            P(("tm", "height")),
        ),
        check_vma=False,
    )
```

```python
import functools
import math

import jax
import jax.numpy as jnp
from jax import lax
from jax.experimental import pallas as pl
from jax.experimental.pallas import tpu as pltpu
from jax.sharding import PartitionSpec as P

EPSILON = 1e-06
MESH = pl.DeviceIdType.MESH
F32 = jnp.float32
BF16 = jnp.bfloat16
NN = (((1,), (0,)), ((), ()))
NT = (((1,), (1,)), ((), ()))
TN = (((0,), (0,)), ((), ()))

SPATIAL_ROWS = 72
TEMPORAL_ROWS = 24
LANES = 128
CHUNKS = (("spatial", 0, 32, 32), ("spatial", 64, 32, 48), ("temporal", 0, 32, 16))


def dot(left, right, dims=NN):
    return lax.dot_general(left, right, dims, preferred_element_type=F32)


def flat(block):
    return block.reshape(-1, block.shape[-1])


def activate(values):
    scale_inv = lax.rsqrt(jnp.mean(values * values, axis=-1, keepdims=True) + EPSILON)
    normed = values * scale_inv
    return normed / (1.0 + jnp.exp(-normed))


def columns(block):
    wide = block.astype(F32)
    zero = jnp.zeros(wide.shape[:-2] + (1,) + wide.shape[-1:], F32)
    axis = wide.ndim - 2
    count = wide.shape[axis]
    before = jnp.concatenate([zero, lax.slice_in_dim(wide, 0, count - 1, axis=axis)], axis=axis)
    after = jnp.concatenate([lax.slice_in_dim(wide, 1, count, axis=axis), zero], axis=axis)
    return before.astype(BF16), block.astype(BF16), after.astype(BF16)


def body(
    sizes, reduce_inside, clip_hbm, cot_hbm, sw_hbm, tw_hbm, out, gclip, gs_out, gt_out,
    clip, sw, tw, in_sem,
    clip_halo, cot_ext, mid_ext, mid_t, gm, gm_halo, act3, gm3, act_t, grad_act, gs, gt, hsend, hrecv, *rest
):
    tm_count, h_count = sizes
    frames, rows, cols, ch = clip.shape
    block = (frames, rows, cols, ch)
    tm = lax.axis_index("tm")
    hh = lax.axis_index("height")
    cells = rows * cols

    cot, cot_next = cot_ext.at[pl.ds(0, frames)], cot_ext.at[pl.ds(frames, frames)]
    mid_prev, mid = mid_ext.at[pl.ds(0, frames)], mid_ext.at[pl.ds(frames, frames)]

    loads = [
        pltpu.make_async_copy(src, dst, in_sem.at[i])
        for i, (src, dst) in enumerate(
            ((clip_hbm, clip), (cot_hbm, cot), (sw_hbm, sw), (tw_hbm, tw))
        )
    ]
    for load in loads:
        load.start()

    up, down = {"height": hh - 1}, {"height": hh + 1}
    before, after = {"tm": tm - 1}, {"tm": tm + 1}
    has_up, has_down = hh > 0, hh < h_count - 1
    has_before, has_after = tm > 0, tm < tm_count - 1

    barrier = pltpu.get_barrier_semaphore()

    def greet(where, who):
        @pl.when(where)
        def _():
            pl.semaphore_signal(barrier, inc=1, device_id=who, device_id_type=MESH)

    sides = ((has_up, up), (has_down, down), (has_before, before), (has_after, after))
    for where, who in sides:
        greet(where, who)
    if reduce_inside:
        core, xx, yy, zz = lax.rem(tm, 2), tm // 2, lax.rem(hh, 2), hh // 2
        by_core = {"tm": xx * 2 + 1 - core}
        by_x = {"tm": (1 - xx) * 2 + core}
        by_y = {"height": zz * 2 + 1 - yy}
        by_z = [{"height": lax.rem(zz + off, 4) * 2 + yy} for off in (1, 2, 3)]
        for who in [by_core, by_x, by_y] + by_z:
            pl.semaphore_signal(barrier, inc=1, device_id=who, device_id_type=MESH)

    greeted = 6 if reduce_inside else 0
    for where, who in sides:
        greeted = greeted + where.astype(jnp.int32)
    pl.semaphore_wait(barrier, greeted)

    def copy(src, dst, slot, who):
        return pltpu.make_async_remote_copy(
            src_ref=src, dst_ref=dst, send_sem=hsend.at[slot], recv_sem=hrecv.at[slot],
            device_id=who, device_id_type=MESH,
        )

    def exchange(slot, src_first, src_last, dst, send_up, send_down):
        return (
            (copy(src_first, dst.at[1], slot, up), has_up, has_down),
            (copy(src_last, dst.at[0], slot + 1, down), has_down, has_up),
        )

    def start(c):
        @pl.when(c[1])
        def _():
            c[0].start()

    def wait_recv(c, target):
        @pl.when(c[2])
        def _():
            c[0].wait_recv()

        @pl.when(jnp.logical_not(c[2]))
        def _():
            target[...] = jnp.zeros(target.shape, target.dtype)

    def wait_send(c):
        @pl.when(c[1])
        def _():
            c[0].wait_send()

    cot_copy = (copy(cot_hbm, cot_next, 0, before), has_before, has_after)
    clip_up, clip_down = exchange(1, clip_hbm.at[:, 0], clip_hbm.at[:, rows - 1], clip_halo, up, down)
    start(clip_up)
    start(clip_down)
    start(cot_copy)

    loads[0].wait()

    def put_act(f, row, values):
        act = activate(values.astype(F32))
        for q, part in enumerate(columns(act)):
            act3[f, row, :, pl.ds(q * ch, ch)] = part

    for f in range(frames):
        for row in range(rows):
            put_act(f, row + 1, clip[f, row])

    def turn_act(r):
        for f in range(frames):
            act_t[pl.ds(r * ch, ch), pl.ds(f * cells, cells)] = flat(
                act3[f, r : r + rows, :, pl.ds(ch, ch)]
            ).T

    turn_act(1)
    wait_recv(clip_up, clip_halo.at[1])
    wait_recv(clip_down, clip_halo.at[0])
    for f in range(frames):
        put_act(f, 0, clip_halo[0, f])
        put_act(f, rows + 1, clip_halo[1, f])

    loads[2].wait()
    total = None
    for r in range(3):
        term = dot(flat(act3[:, r : r + rows]), flat(sw[r]))
        total = term if total is None else total + term
    mid_ext[frames:] = total.astype(BF16).reshape(block)
    mid_copy = (copy(mid, mid_prev, 3, after), has_after, has_before)
    start(mid_copy)

    turn_act(0)
    turn_act(2)

    loads[1].wait()
    loads[3].wait()
    wait_recv(cot_copy, cot_next)

    def put_gm(f, row, values):
        shifts = columns(values)
        for q in range(3):
            gm3[f, row, :, pl.ds(q * ch, ch)] = shifts[2 - q]

    total = None
    for k in range(3):
        term = dot(flat(cot_ext[k : k + frames]), tw[k], NT)
        total = term if total is None else total + term
    value = total.astype(BF16).reshape(block)
    gm[...] = value
    gm_up, gm_down = exchange(4, gm.at[:, 0], gm.at[:, rows - 1], gm_halo, up, down)
    start(gm_up)
    start(gm_down)
    for f in range(frames):
        for row in range(rows):
            put_gm(f, row + 1, value[f, row])

    for q in range(3):
        total = dot(act_t[...], flat(gm3[:, 1 : 1 + rows, :, pl.ds(q * ch, ch)]))
        for r in range(3):
            gs[pl.ds((r * 3 + q) * ch, ch), :] = total[r * ch : (r + 1) * ch]

    def turn_mid(t):
        mid_t[:, pl.ds(t * cells, cells)] = flat(mid_ext[t]).T

    def do_temporal():
        for t in range(frames, 2 * frames):
            turn_mid(t)
        wait_recv(mid_copy, mid_prev)
        for t in range(frames):
            turn_mid(t)
        left = jnp.concatenate(
            [mid_t[:, pl.ds((frames - k) * cells, frames * cells)] for k in range(3)], axis=0
        )
        gt[...] = dot(left, flat(cot_ext[:frames]))

    def do_output():
        total = flat(clip[...]).astype(F32)
        for k in range(3):
            total = total + dot(flat(mid_ext[frames - k : 2 * frames - k]), tw[k])
        out[...] = total.astype(BF16).reshape(block)

    def do_gm_halo():
        wait_recv(gm_up, gm_halo.at[1])
        wait_recv(gm_down, gm_halo.at[0])
        for f in range(frames):
            put_gm(f, 0, gm_halo[0, f])
            put_gm(f, rows + 1, gm_halo[1, f])

    def do_grad_act(r):
        total = None
        for q in range(3):
            left = flat(gm3[:, 2 - r : 2 - r + rows, :, pl.ds(q * ch, ch)])
            term = dot(left, sw[r, q], NT)
            total = term if total is None else total + term
        if r == 0:
            grad_act[...] = total
        else:
            grad_act[...] += total

    def do_grad_clip(f):
        values = flat(clip[f]).astype(F32)
        scale_inv = lax.rsqrt(jnp.mean(values * values, axis=-1, keepdims=True) + EPSILON)
        normed = values * scale_inv
        gate = 1.0 / (1.0 + jnp.exp(-normed))
        inner = grad_act[pl.ds(f * cells, cells), :] * (gate * (1.0 + normed * (1.0 - gate)))
        slope = scale_inv * (
            inner - normed * jnp.mean(inner * normed, axis=-1, keepdims=True)
        )
        total = flat(cot_ext[f]).astype(F32) + slope
        gclip[f] = total.astype(BF16).reshape(rows, cols, ch)

    scale = 1.0 / math.sqrt(frames * tm_count * rows * h_count * cols)

    if not reduce_inside:
        do_temporal()
        do_output()
        do_gm_halo()
        for r in range(3):
            do_grad_act(r)
        for f in range(frames):
            do_grad_clip(f)
        gs_out[...] = gs[...] * scale
        gt_out[...] = gt[...] * scale
    else:
        rsend, rrecv = rest[-2:]
        bufs = [rest[11 * i : 11 * i + 11] for i in range(len(CHUNKS))]

        def rcopy(src, dst, slot, who):
            return pltpu.make_async_remote_copy(
                src_ref=src, dst_ref=dst, send_sem=rsend.at[slot], recv_sem=rrecv.at[slot],
                device_id=who, device_id_type=MESH,
            )

        def piece(chunk, d):
            kind, first, a, b = chunk
            ref, count = (gs, SPATIAL_ROWS) if kind == "spatial" else (gt, TEMPORAL_ROWS)
            block = ref[pl.ds(pl.multiple_of(d * count, 8), count), :]
            both = jnp.concatenate([block[:, :LANES], block[:, LANES:]], axis=0)
            return both[first : first + a + b]

        def each(count):
            def run(step):
                def four(j, carry):
                    for i in range(4):
                        step(j * 4 + i)
                    return carry

                lax.fori_loop(0, count // 4, four, 0)

            return run

        def owner(j, which):
            return ((j // 8) * 2 + which) * 8 + lax.rem(j, 8)

        def stage_core(i):
            send0, recv0 = bufs[i][:2]

            @each(16)
            def _(j):
                send0[j] = piece(CHUNKS[i], owner(j, 1 - core)).astype(BF16)

            c = rcopy(send0, recv0, 8 * i, by_core)
            c.start()
            return [c]

        def stage_one(i):
            a = CHUNKS[i][2]
            send0, recv0, part, send_a, recv_a, send_b, recv_b = bufs[i][:7]

            @each(16)
            def _(j):
                part[j] = piece(CHUNKS[i], owner(j, core)) + recv0[j].astype(F32)

            @each(8)
            def _(j):
                send_a[j] = part[(1 - xx) * 8 + j, :a].astype(BF16)
                send_b[j] = part[j * 2 + 1 - yy, a:].astype(BF16)

            cs = [
                rcopy(send_a, recv_a, 8 * i + 1, by_x),
                rcopy(send_b, recv_b, 8 * i + 2, by_y),
            ]
            for c in cs:
                c.start()
            return cs

        def stage_two(i):
            a = CHUNKS[i][2]
            part, _, recv_a, _, recv_b, send_a2, recv_a2, send_b2, recv_b2 = bufs[i][2:11]

            @each(4)
            def _(j):
                away = j * 2 + 1 - yy
                send_a2[j] = (part[xx * 8 + away, :a] + recv_a[away].astype(F32)).astype(BF16)
                far = (1 - xx) * 4 + j
                send_b2[j] = (part[far * 2 + yy, a:] + recv_b[far].astype(F32)).astype(BF16)

            cs = [
                rcopy(send_a2, recv_a2, 8 * i + 3, by_y),
                rcopy(send_b2, recv_b2, 8 * i + 4, by_x),
            ]
            for c in cs:
                c.start()
            return cs

        z_bufs = rest[11 * len(CHUNKS) : -2]

        def stage_z(i):
            a = CHUNKS[i][2]
            part, _, recv_a, _, recv_b, _, recv_a2, _, recv_b2 = bufs[i][2:11]
            total_z, send_z, recv_z = z_bufs[3 * i : 3 * i + 3]

            @each(4)
            def _(j):
                near = j * 2 + yy
                first = part[xx * 8 + near, :a] + recv_a[near].astype(F32) + recv_a2[j].astype(F32)
                last = (
                    part[xx * 8 + near, a:] + recv_b[xx * 4 + j].astype(F32) + recv_b2[j].astype(F32)
                )
                value = jnp.concatenate([first, last], axis=0)
                total_z[j] = value
                send_z[j] = value.astype(BF16)

            cs = [
                rcopy(
                    send_z.at[lax.rem(zz + off, 4)], recv_z.at[off - 1], 8 * i + 4 + off, by_z[off - 1]
                )
                for off in (1, 2, 3)
            ]
            for c in cs:
                c.start()
            return cs

        def final(i):
            total_z, _, recv_z = z_bufs[3 * i : 3 * i + 3]
            value = total_z[zz]
            for off in range(3):
                value = value + recv_z[off].astype(F32)
            return value * scale

        def finish(copies):
            for c in copies:
                c.wait()

        def place(ref, value, count):
            ref[pl.ds(0, count, stride=2), :] = value[:count]
            ref[pl.ds(1, count, stride=2), :] = value[count:]

        spatial = (0, 1)
        flight = {i: stage_core(i) for i in spatial}
        do_temporal()
        flight[2] = stage_core(2)

        def advance(i, stage):
            finish(flight[i])
            flight[i] = stage(i)

        for i in range(len(CHUNKS)):
            advance(i, stage_one)
        do_output()
        do_gm_halo()
        advance(0, stage_two)
        do_grad_act(0)
        advance(1, stage_two)
        do_grad_act(1)
        advance(2, stage_two)
        advance(0, stage_z)
        do_grad_act(2)
        advance(1, stage_z)
        do_grad_clip(0)
        advance(2, stage_z)
        for f in range(1, frames):
            do_grad_clip(f)
        done = []
        for i in range(len(CHUNKS)):
            finish(flight[i])
            done.append(final(i))
        place(gs_out, jnp.concatenate(done[:2], axis=0), SPATIAL_ROWS)
        place(gt_out, done[2], TEMPORAL_ROWS)

    for c in (clip_up, clip_down, cot_copy, mid_copy, gm_up, gm_down):
        wait_send(c)


def hand_on(*refs):
    count = len(refs) // 2
    copies = [
        pltpu.make_async_copy(refs[i], refs[count + i], refs[-1].at[i]) for i in range(count)
    ]
    for c in copies:
        c.start()
    for c in copies:
        c.wait()


def handed_on(*arrays):
    place = pl.BlockSpec(memory_space=pltpu.HBM)
    return pl.pallas_call(
        hand_on,
        out_shape=tuple(jax.ShapeDtypeStruct(x.shape, x.dtype) for x in arrays),
        in_specs=[pl.BlockSpec(memory_space=pltpu.VMEM)] * len(arrays),
        out_specs=(place,) * len(arrays),
        scratch_shapes=[pltpu.SemaphoreType.DMA((len(arrays),))],
        compiler_params=pltpu.CompilerParams(vmem_limit_bytes=4 * 1024 * 1024),
        name="hand_on",
    )(*arrays)


def shards(sizes, clip, cot, sw, tw):
    tm_count, h_count = sizes
    frames, rows, cols, ch = clip.shape
    inside = sizes == (4, 8) and ch == 256 and frames == 2
    wide = (frames, rows + 2, cols, 3 * ch)
    edge = (2, frames, cols, ch)
    vmem = pl.BlockSpec(memory_space=pltpu.VMEM)
    scratch = [pltpu.VMEM(x.shape, x.dtype) for x in (clip, sw, tw)]
    scratch += [
        pltpu.SemaphoreType.DMA((4,)),
        pltpu.VMEM(edge, BF16),
        pltpu.VMEM((2 * frames, rows, cols, ch), BF16),
        pltpu.VMEM((2 * frames, rows, cols, ch), BF16),
        pltpu.VMEM((ch, 2 * frames * rows * cols), BF16),
        pltpu.VMEM(clip.shape, BF16),
        pltpu.VMEM(edge, BF16),
        pltpu.VMEM(wide, BF16),
        pltpu.VMEM(wide, BF16),
        pltpu.VMEM((3 * ch, frames * rows * cols), BF16),
        pltpu.VMEM((frames * rows * cols, ch), F32),
        pltpu.VMEM((9 * ch, ch), F32),
        pltpu.VMEM((3 * ch, ch), F32),
        pltpu.SemaphoreType.DMA((6,)),
        pltpu.SemaphoreType.DMA((6,)),
    ]
    gs_shape, gt_shape = (9 * ch, ch), (3 * ch, ch)
    if inside:
        gs_shape, gt_shape = (2 * SPATIAL_ROWS, LANES), (2 * TEMPORAL_ROWS, LANES)
        for _, _, a, b in CHUNKS:
            n = a + b
            scratch += [pltpu.VMEM((16, n, LANES), BF16)] * 2
            scratch += [pltpu.VMEM((16, n, LANES), F32)]
            scratch += [pltpu.VMEM((8, a, LANES), BF16)] * 2
            scratch += [pltpu.VMEM((8, b, LANES), BF16)] * 2
            scratch += [pltpu.VMEM((4, a, LANES), BF16)] * 2
            scratch += [pltpu.VMEM((4, b, LANES), BF16)] * 2
        for _, _, a, b in CHUNKS:
            n = a + b
            scratch += [
                pltpu.VMEM((4, n, LANES), F32),
                pltpu.VMEM((4, n, LANES), BF16),
                pltpu.VMEM((3, n, LANES), BF16),
            ]
        scratch += [pltpu.SemaphoreType.DMA((8 * len(CHUNKS),))] * 2
    out, gclip, gs, gt = pl.pallas_call(
        functools.partial(body, sizes, inside),
        out_shape=(
            jax.ShapeDtypeStruct(clip.shape, BF16),
            jax.ShapeDtypeStruct(clip.shape, BF16),
            jax.ShapeDtypeStruct(gs_shape, F32),
            jax.ShapeDtypeStruct(gt_shape, F32),
        ),
        in_specs=[pl.BlockSpec(memory_space=pltpu.HBM)] * 4,
        out_specs=(vmem,) * 4,
        scratch_shapes=scratch,
        compiler_params=pltpu.CompilerParams(
            collective_id=0, has_side_effects=True, vmem_limit_bytes=531 * 1024 * 1024 // 10
        ),
        name="section",
    )(clip, cot, sw, tw)
    if inside:
        out, gclip, gs, gt = handed_on(out, gclip, gs, gt)
    gs, gt = gs.reshape(-1), gt.reshape(-1)
    if not inside:
        gs, gt = (
            lax.psum_scatter(gs, ("tm", "height"), scatter_dimension=0, tiled=True),
            lax.psum_scatter(gt, ("tm", "height"), scatter_dimension=0, tiled=True),
        )
    return out, gclip, gs, gt


def solution(mesh):
    sizes = (mesh.shape["tm"], mesh.shape["height"])
    return jax.shard_map(
        functools.partial(shards, sizes),
        mesh=mesh,
        in_specs=(P("tm", "height", None, None), P("tm", "height", None, None), P(), P()),
        out_specs=(
            P("tm", "height", None, None),
            P("tm", "height", None, None),
            P(("tm", "height")),
            P(("tm", "height")),
        ),
        check_vma=False,
    )
```

```python
import functools
import math

import jax
import jax.numpy as jnp
from jax import lax
from jax.experimental import pallas as pl
from jax.experimental.pallas import tpu as pltpu
from jax.sharding import PartitionSpec as P

EPSILON = 1e-06
MESH = pl.DeviceIdType.MESH
F32 = jnp.float32
BF16 = jnp.bfloat16
NN = (((1,), (0,)), ((), ()))
NT = (((1,), (1,)), ((), ()))
TN = (((0,), (0,)), ((), ()))

SPATIAL_ROWS = 72
TEMPORAL_ROWS = 24
LANES = 128
CHUNKS = (("spatial", 0, 64, 80), ("temporal", 0, 32, 16))


def dot(left, right, dims=NN):
    return lax.dot_general(left, right, dims, preferred_element_type=F32)


def flat(block):
    return block.reshape(-1, block.shape[-1])


def activate(values):
    scale_inv = lax.rsqrt(jnp.mean(values * values, axis=-1, keepdims=True) + EPSILON)
    normed = values * scale_inv
    return normed / (1.0 + jnp.exp(-normed))


def columns(block):
    wide = block.astype(F32)
    zero = jnp.zeros(wide.shape[:-2] + (1,) + wide.shape[-1:], F32)
    axis = wide.ndim - 2
    count = wide.shape[axis]
    before = jnp.concatenate([zero, lax.slice_in_dim(wide, 0, count - 1, axis=axis)], axis=axis)
    after = jnp.concatenate([lax.slice_in_dim(wide, 1, count, axis=axis), zero], axis=axis)
    return before.astype(BF16), block.astype(BF16), after.astype(BF16)


def body(
    sizes, reduce_inside, clip_hbm, cot_hbm, sw_hbm, tw_hbm, out, gclip, gs_out, gt_out,
    clip, sw, tw, in_sem,
    clip_halo, cot_ext, mid_ext, mid_t, gm, gm_halo, act3, gm3, act_t, grad_act, gs, gt, hsend, hrecv, *rest
):
    tm_count, h_count = sizes
    frames, rows, cols, ch = clip.shape
    block = (frames, rows, cols, ch)
    tm = lax.axis_index("tm")
    hh = lax.axis_index("height")
    cells = rows * cols

    cot, cot_next = cot_ext.at[pl.ds(0, frames)], cot_ext.at[pl.ds(frames, frames)]
    mid_prev, mid = mid_ext.at[pl.ds(0, frames)], mid_ext.at[pl.ds(frames, frames)]

    loads = [
        pltpu.make_async_copy(src, dst, in_sem.at[i])
        for i, (src, dst) in enumerate(
            ((clip_hbm, clip), (cot_hbm, cot), (sw_hbm, sw), (tw_hbm, tw))
        )
    ]
    for load in loads:
        load.start()

    up, down = {"height": hh - 1}, {"height": hh + 1}
    before, after = {"tm": tm - 1}, {"tm": tm + 1}
    has_up, has_down = hh > 0, hh < h_count - 1
    has_before, has_after = tm > 0, tm < tm_count - 1

    barrier = pltpu.get_barrier_semaphore()

    def greet(where, who):
        @pl.when(where)
        def _():
            pl.semaphore_signal(barrier, inc=1, device_id=who, device_id_type=MESH)

    sides = ((has_up, up), (has_down, down), (has_before, before), (has_after, after))
    for where, who in sides:
        greet(where, who)
    if reduce_inside:
        core, xx, yy, zz = lax.rem(tm, 2), tm // 2, lax.rem(hh, 2), hh // 2
        by_core = {"tm": xx * 2 + 1 - core}
        by_x = {"tm": (1 - xx) * 2 + core}
        by_y = {"height": zz * 2 + 1 - yy}
        by_z = [{"height": lax.rem(zz + off, 4) * 2 + yy} for off in (1, 2, 3)]
        for who in [by_core, by_x, by_y] + by_z:
            pl.semaphore_signal(barrier, inc=1, device_id=who, device_id_type=MESH)

    greeted = 6 if reduce_inside else 0
    for where, who in sides:
        greeted = greeted + where.astype(jnp.int32)
    pl.semaphore_wait(barrier, greeted)

    def copy(src, dst, slot, who):
        return pltpu.make_async_remote_copy(
            src_ref=src, dst_ref=dst, send_sem=hsend.at[slot], recv_sem=hrecv.at[slot],
            device_id=who, device_id_type=MESH,
        )

    def exchange(slot, src_first, src_last, dst, send_up, send_down):
        return (
            (copy(src_first, dst.at[1], slot, up), has_up, has_down),
            (copy(src_last, dst.at[0], slot + 1, down), has_down, has_up),
        )

    def start(c):
        @pl.when(c[1])
        def _():
            c[0].start()

    def wait_recv(c, target):
        @pl.when(c[2])
        def _():
            c[0].wait_recv()

        @pl.when(jnp.logical_not(c[2]))
        def _():
            target[...] = jnp.zeros(target.shape, target.dtype)

    def wait_send(c):
        @pl.when(c[1])
        def _():
            c[0].wait_send()

    cot_copy = (copy(cot_hbm, cot_next, 0, before), has_before, has_after)
    clip_up, clip_down = exchange(1, clip_hbm.at[:, 0], clip_hbm.at[:, rows - 1], clip_halo, up, down)
    start(clip_up)
    start(clip_down)
    start(cot_copy)

    loads[0].wait()

    def put_act(f, row, values):
        act = activate(values.astype(F32))
        for q, part in enumerate(columns(act)):
            act3[f, row, :, pl.ds(q * ch, ch)] = part

    for f in range(frames):
        for row in range(rows):
            put_act(f, row + 1, clip[f, row])

    def turn_act(r):
        for f in range(frames):
            act_t[pl.ds(r * ch, ch), pl.ds(f * cells, cells)] = flat(
                act3[f, r : r + rows, :, pl.ds(ch, ch)]
            ).T

    turn_act(1)
    wait_recv(clip_up, clip_halo.at[1])
    wait_recv(clip_down, clip_halo.at[0])
    for f in range(frames):
        put_act(f, 0, clip_halo[0, f])
        put_act(f, rows + 1, clip_halo[1, f])

    loads[2].wait()
    total = None
    for r in range(3):
        term = dot(flat(act3[:, r : r + rows]), flat(sw[r]))
        total = term if total is None else total + term
    mid_ext[frames:] = total.astype(BF16).reshape(block)
    mid_copy = (copy(mid, mid_prev, 3, after), has_after, has_before)
    start(mid_copy)

    turn_act(0)
    turn_act(2)

    loads[1].wait()
    loads[3].wait()
    wait_recv(cot_copy, cot_next)

    def put_gm(f, row, values):
        shifts = columns(values)
        for q in range(3):
            gm3[f, row, :, pl.ds(q * ch, ch)] = shifts[2 - q]

    total = None
    for k in range(3):
        term = dot(flat(cot_ext[k : k + frames]), tw[k], NT)
        total = term if total is None else total + term
    value = total.astype(BF16).reshape(block)
    gm[...] = value
    gm_up, gm_down = exchange(4, gm.at[:, 0], gm.at[:, rows - 1], gm_halo, up, down)
    start(gm_up)
    start(gm_down)
    for f in range(frames):
        for row in range(rows):
            put_gm(f, row + 1, value[f, row])

    for q in range(3):
        total = dot(act_t[...], flat(gm3[:, 1 : 1 + rows, :, pl.ds(q * ch, ch)]))
        for r in range(3):
            gs[pl.ds((r * 3 + q) * ch, ch), :] = total[r * ch : (r + 1) * ch]

    def turn_mid(t):
        mid_t[:, pl.ds(t * cells, cells)] = flat(mid_ext[t]).T

    def do_temporal():
        for t in range(frames, 2 * frames):
            turn_mid(t)
        wait_recv(mid_copy, mid_prev)
        for t in range(frames):
            turn_mid(t)
        left = jnp.concatenate(
            [mid_t[:, pl.ds((frames - k) * cells, frames * cells)] for k in range(3)], axis=0
        )
        gt[...] = dot(left, flat(cot_ext[:frames]))

    def do_output():
        total = flat(clip[...]).astype(F32)
        for k in range(3):
            total = total + dot(flat(mid_ext[frames - k : 2 * frames - k]), tw[k])
        out[...] = total.astype(BF16).reshape(block)

    def do_gm_halo():
        wait_recv(gm_up, gm_halo.at[1])
        wait_recv(gm_down, gm_halo.at[0])
        for f in range(frames):
            put_gm(f, 0, gm_halo[0, f])
            put_gm(f, rows + 1, gm_halo[1, f])

    def do_grad_act(r):
        total = None
        for q in range(3):
            left = flat(gm3[:, 2 - r : 2 - r + rows, :, pl.ds(q * ch, ch)])
            term = dot(left, sw[r, q], NT)
            total = term if total is None else total + term
        if r == 0:
            grad_act[...] = total
        else:
            grad_act[...] += total

    def do_grad_clip(f):
        values = flat(clip[f]).astype(F32)
        scale_inv = lax.rsqrt(jnp.mean(values * values, axis=-1, keepdims=True) + EPSILON)
        normed = values * scale_inv
        gate = 1.0 / (1.0 + jnp.exp(-normed))
        inner = grad_act[pl.ds(f * cells, cells), :] * (gate * (1.0 + normed * (1.0 - gate)))
        slope = scale_inv * (
            inner - normed * jnp.mean(inner * normed, axis=-1, keepdims=True)
        )
        total = flat(cot_ext[f]).astype(F32) + slope
        gclip[f] = total.astype(BF16).reshape(rows, cols, ch)

    scale = 1.0 / math.sqrt(frames * tm_count * rows * h_count * cols)

    if not reduce_inside:
        do_temporal()
        do_output()
        do_gm_halo()
        for r in range(3):
            do_grad_act(r)
        for f in range(frames):
            do_grad_clip(f)
        gs_out[...] = gs[...] * scale
        gt_out[...] = gt[...] * scale
    else:
        rsend, rrecv = rest[-2:]
        bufs = [rest[11 * i : 11 * i + 11] for i in range(len(CHUNKS))]

        def rcopy(src, dst, slot, who):
            return pltpu.make_async_remote_copy(
                src_ref=src, dst_ref=dst, send_sem=rsend.at[slot], recv_sem=rrecv.at[slot],
                device_id=who, device_id_type=MESH,
            )

        def piece(chunk, d):
            kind, first, a, b = chunk
            ref, count = (gs, SPATIAL_ROWS) if kind == "spatial" else (gt, TEMPORAL_ROWS)
            block = ref[pl.ds(pl.multiple_of(d * count, 8), count), :]
            both = jnp.concatenate([block[:, :LANES], block[:, LANES:]], axis=0)
            return both[first : first + a + b]

        def each(count):
            def run(step):
                def four(j, carry):
                    for i in range(4):
                        step(j * 4 + i)
                    return carry

                lax.fori_loop(0, count // 4, four, 0)

            return run

        def owner(j, which):
            return ((j // 8) * 2 + which) * 8 + lax.rem(j, 8)

        def stage_core(i):
            send0, recv0 = bufs[i][:2]

            @each(16)
            def _(j):
                send0[j] = piece(CHUNKS[i], owner(j, 1 - core)).astype(BF16)

            c = rcopy(send0, recv0, 8 * i, by_core)
            c.start()
            return [c]

        def stage_one(i):
            a = CHUNKS[i][2]
            send0, recv0, part, send_a, recv_a, send_b, recv_b = bufs[i][:7]

            @each(16)
            def _(j):
                part[j] = piece(CHUNKS[i], owner(j, core)) + recv0[j].astype(F32)

            @each(8)
            def _(j):
                send_a[j] = part[(1 - xx) * 8 + j, :a].astype(BF16)
                send_b[j] = part[j * 2 + 1 - yy, a:].astype(BF16)

            cs = [
                rcopy(send_a, recv_a, 8 * i + 1, by_x),
                rcopy(send_b, recv_b, 8 * i + 2, by_y),
            ]
            for c in cs:
                c.start()
            return cs

        def stage_two(i):
            a = CHUNKS[i][2]
            part, _, recv_a, _, recv_b, send_a2, recv_a2, send_b2, recv_b2 = bufs[i][2:11]

            @each(4)
            def _(j):
                away = j * 2 + 1 - yy
                send_a2[j] = (part[xx * 8 + away, :a] + recv_a[away].astype(F32)).astype(BF16)
                far = (1 - xx) * 4 + j
                send_b2[j] = (part[far * 2 + yy, a:] + recv_b[far].astype(F32)).astype(BF16)

            cs = [
                rcopy(send_a2, recv_a2, 8 * i + 3, by_y),
                rcopy(send_b2, recv_b2, 8 * i + 4, by_x),
            ]
            for c in cs:
                c.start()
            return cs

        z_bufs = rest[11 * len(CHUNKS) : -2]

        def stage_z(i):
            a = CHUNKS[i][2]
            part, _, recv_a, _, recv_b, _, recv_a2, _, recv_b2 = bufs[i][2:11]
            total_z, send_z, recv_z = z_bufs[3 * i : 3 * i + 3]

            @each(4)
            def _(j):
                near = j * 2 + yy
                first = part[xx * 8 + near, :a] + recv_a[near].astype(F32) + recv_a2[j].astype(F32)
                last = (
                    part[xx * 8 + near, a:] + recv_b[xx * 4 + j].astype(F32) + recv_b2[j].astype(F32)
                )
                value = jnp.concatenate([first, last], axis=0)
                total_z[j] = value
                send_z[j] = value.astype(BF16)

            cs = [
                rcopy(
                    send_z.at[lax.rem(zz + off, 4)], recv_z.at[off - 1], 8 * i + 4 + off, by_z[off - 1]
                )
                for off in (1, 2, 3)
            ]
            for c in cs:
                c.start()
            return cs

        def final(i):
            total_z, _, recv_z = z_bufs[3 * i : 3 * i + 3]
            value = total_z[zz]
            for off in range(3):
                value = value + recv_z[off].astype(F32)
            return value * scale

        def finish(copies):
            for c in copies:
                c.wait()

        def place(ref, value, count):
            ref[pl.ds(0, count, stride=2), :] = value[:count]
            ref[pl.ds(1, count, stride=2), :] = value[count:]

        flight = {0: stage_core(0)}
        do_temporal()
        flight[1] = stage_core(1)

        def advance(i, stage):
            finish(flight[i])
            flight[i] = stage(i)

        advance(0, stage_one)
        advance(1, stage_one)
        do_output()
        do_gm_halo()
        do_grad_act(0)
        advance(0, stage_two)
        do_grad_act(1)
        advance(1, stage_two)
        advance(0, stage_z)
        do_grad_act(2)
        do_grad_clip(0)
        advance(1, stage_z)
        for f in range(1, frames):
            do_grad_clip(f)
        done = []
        for i in range(len(CHUNKS)):
            finish(flight[i])
            done.append(final(i))
        place(gs_out, done[0], SPATIAL_ROWS)
        place(gt_out, done[1], TEMPORAL_ROWS)

    for c in (clip_up, clip_down, cot_copy, mid_copy, gm_up, gm_down):
        wait_send(c)


def hand_on(*refs):
    count = len(refs) // 2
    copies = [
        pltpu.make_async_copy(refs[i], refs[count + i], refs[-1].at[i]) for i in range(count)
    ]
    for c in copies:
        c.start()
    for c in copies:
        c.wait()


def handed_on(*arrays):
    place = pl.BlockSpec(memory_space=pltpu.HBM)
    return pl.pallas_call(
        hand_on,
        out_shape=tuple(jax.ShapeDtypeStruct(x.shape, x.dtype) for x in arrays),
        in_specs=[pl.BlockSpec(memory_space=pltpu.VMEM)] * len(arrays),
        out_specs=(place,) * len(arrays),
        scratch_shapes=[pltpu.SemaphoreType.DMA((len(arrays),))],
        compiler_params=pltpu.CompilerParams(vmem_limit_bytes=4 * 1024 * 1024),
        name="hand_on",
    )(*arrays)


def shards(sizes, clip, cot, sw, tw):
    tm_count, h_count = sizes
    frames, rows, cols, ch = clip.shape
    inside = sizes == (4, 8) and ch == 256 and frames == 2
    wide = (frames, rows + 2, cols, 3 * ch)
    edge = (2, frames, cols, ch)
    vmem = pl.BlockSpec(memory_space=pltpu.VMEM)
    scratch = [pltpu.VMEM(x.shape, x.dtype) for x in (clip, sw, tw)]
    scratch += [
        pltpu.SemaphoreType.DMA((4,)),
        pltpu.VMEM(edge, BF16),
        pltpu.VMEM((2 * frames, rows, cols, ch), BF16),
        pltpu.VMEM((2 * frames, rows, cols, ch), BF16),
        pltpu.VMEM((ch, 2 * frames * rows * cols), BF16),
        pltpu.VMEM(clip.shape, BF16),
        pltpu.VMEM(edge, BF16),
        pltpu.VMEM(wide, BF16),
        pltpu.VMEM(wide, BF16),
        pltpu.VMEM((3 * ch, frames * rows * cols), BF16),
        pltpu.VMEM((frames * rows * cols, ch), F32),
        pltpu.VMEM((9 * ch, ch), F32),
        pltpu.VMEM((3 * ch, ch), F32),
        pltpu.SemaphoreType.DMA((6,)),
        pltpu.SemaphoreType.DMA((6,)),
    ]
    gs_shape, gt_shape = (9 * ch, ch), (3 * ch, ch)
    if inside:
        gs_shape, gt_shape = (2 * SPATIAL_ROWS, LANES), (2 * TEMPORAL_ROWS, LANES)
        for _, _, a, b in CHUNKS:
            n = a + b
            scratch += [pltpu.VMEM((16, n, LANES), BF16)] * 2
            scratch += [pltpu.VMEM((16, n, LANES), F32)]
            scratch += [pltpu.VMEM((8, a, LANES), BF16)] * 2
            scratch += [pltpu.VMEM((8, b, LANES), BF16)] * 2
            scratch += [pltpu.VMEM((4, a, LANES), BF16)] * 2
            scratch += [pltpu.VMEM((4, b, LANES), BF16)] * 2
        for _, _, a, b in CHUNKS:
            n = a + b
            scratch += [
                pltpu.VMEM((4, n, LANES), F32),
                pltpu.VMEM((4, n, LANES), BF16),
                pltpu.VMEM((3, n, LANES), BF16),
            ]
        scratch += [pltpu.SemaphoreType.DMA((8 * len(CHUNKS),))] * 2
    out, gclip, gs, gt = pl.pallas_call(
        functools.partial(body, sizes, inside),
        out_shape=(
            jax.ShapeDtypeStruct(clip.shape, BF16),
            jax.ShapeDtypeStruct(clip.shape, BF16),
            jax.ShapeDtypeStruct(gs_shape, F32),
            jax.ShapeDtypeStruct(gt_shape, F32),
        ),
        in_specs=[pl.BlockSpec(memory_space=pltpu.HBM)] * 4,
        out_specs=(vmem,) * 4,
        scratch_shapes=scratch,
        compiler_params=pltpu.CompilerParams(
            collective_id=0, has_side_effects=True, vmem_limit_bytes=531 * 1024 * 1024 // 10
        ),
        name="section",
    )(clip, cot, sw, tw)
    if inside:
        out, gclip, gs, gt = handed_on(out, gclip, gs, gt)
    gs, gt = gs.reshape(-1), gt.reshape(-1)
    if not inside:
        gs, gt = (
            lax.psum_scatter(gs, ("tm", "height"), scatter_dimension=0, tiled=True),
            lax.psum_scatter(gt, ("tm", "height"), scatter_dimension=0, tiled=True),
        )
    return out, gclip, gs, gt


def solution(mesh):
    sizes = (mesh.shape["tm"], mesh.shape["height"])
    return jax.shard_map(
        functools.partial(shards, sizes),
        mesh=mesh,
        in_specs=(P("tm", "height", None, None), P("tm", "height", None, None), P(), P()),
        out_specs=(
            P("tm", "height", None, None),
            P("tm", "height", None, None),
            P(("tm", "height")),
            P(("tm", "height")),
        ),
        check_vma=False,
    )
```

```python
import functools
import math

import jax
import jax.numpy as jnp
from jax import lax
from jax.experimental import pallas as pl
from jax.experimental.pallas import tpu as pltpu
from jax.sharding import PartitionSpec as P

EPSILON = 1e-06
MESH = pl.DeviceIdType.MESH
F32 = jnp.float32
BF16 = jnp.bfloat16
NN = (((1,), (0,)), ((), ()))
NT = (((1,), (1,)), ((), ()))
TN = (((0,), (0,)), ((), ()))

SPATIAL_ROWS = 72
TEMPORAL_ROWS = 24
LANES = 128
CHUNKS = (("spatial", 0, 32, 32), ("spatial", 64, 32, 48), ("temporal", 0, 16, 32))


def dot(left, right, dims=NN):
    return lax.dot_general(left, right, dims, preferred_element_type=F32)


def flat(block):
    return block.reshape(-1, block.shape[-1])


def activate(values):
    scale_inv = lax.rsqrt(jnp.mean(values * values, axis=-1, keepdims=True) + EPSILON)
    normed = values * scale_inv
    return normed / (1.0 + jnp.exp(-normed))


def columns(block):
    wide = block.astype(F32)
    zero = jnp.zeros(wide.shape[:-2] + (1,) + wide.shape[-1:], F32)
    axis = wide.ndim - 2
    count = wide.shape[axis]
    before = jnp.concatenate([zero, lax.slice_in_dim(wide, 0, count - 1, axis=axis)], axis=axis)
    after = jnp.concatenate([lax.slice_in_dim(wide, 1, count, axis=axis), zero], axis=axis)
    return before.astype(BF16), block.astype(BF16), after.astype(BF16)


def body(
    sizes, reduce_inside, clip_hbm, cot_hbm, sw_hbm, tw_hbm, out, gclip, gs_out, gt_out,
    clip, sw, tw, in_sem,
    clip_halo, cot_ext, mid_ext, mid_t, gm, gm_halo, act3, gm3, act_t, grad_act, gs, gt, hsend, hrecv, *rest
):
    tm_count, h_count = sizes
    frames, rows, cols, ch = clip.shape
    block = (frames, rows, cols, ch)
    tm = lax.axis_index("tm")
    hh = lax.axis_index("height")
    cells = rows * cols

    cot, cot_next = cot_ext.at[pl.ds(0, frames)], cot_ext.at[pl.ds(frames, frames)]
    mid_prev, mid = mid_ext.at[pl.ds(0, frames)], mid_ext.at[pl.ds(frames, frames)]

    loads = [
        pltpu.make_async_copy(src, dst, in_sem.at[i])
        for i, (src, dst) in enumerate(
            ((clip_hbm, clip), (cot_hbm, cot), (sw_hbm, sw), (tw_hbm, tw))
        )
    ]
    for load in loads:
        load.start()

    up, down = {"height": hh - 1}, {"height": hh + 1}
    before, after = {"tm": tm - 1}, {"tm": tm + 1}
    has_up, has_down = hh > 0, hh < h_count - 1
    has_before, has_after = tm > 0, tm < tm_count - 1

    barrier = pltpu.get_barrier_semaphore()

    def greet(where, who):
        @pl.when(where)
        def _():
            pl.semaphore_signal(barrier, inc=1, device_id=who, device_id_type=MESH)

    sides = ((has_up, up), (has_down, down), (has_before, before), (has_after, after))
    for where, who in sides:
        greet(where, who)
    if reduce_inside:
        core, xx, yy, zz = lax.rem(tm, 2), tm // 2, lax.rem(hh, 2), hh // 2
        by_core = {"tm": xx * 2 + 1 - core}
        by_x = {"tm": (1 - xx) * 2 + core}
        by_y = {"height": zz * 2 + 1 - yy}
        by_z = [{"height": lax.rem(zz + off, 4) * 2 + yy} for off in (1, 2, 3)]
        for who in [by_core, by_x, by_y] + by_z:
            pl.semaphore_signal(barrier, inc=1, device_id=who, device_id_type=MESH)

    greeted = 6 if reduce_inside else 0
    for where, who in sides:
        greeted = greeted + where.astype(jnp.int32)
    pl.semaphore_wait(barrier, greeted)

    def copy(src, dst, slot, who):
        return pltpu.make_async_remote_copy(
            src_ref=src, dst_ref=dst, send_sem=hsend.at[slot], recv_sem=hrecv.at[slot],
            device_id=who, device_id_type=MESH,
        )

    def exchange(slot, src_first, src_last, dst, send_up, send_down):
        return (
            (copy(src_first, dst.at[1], slot, up), has_up, has_down),
            (copy(src_last, dst.at[0], slot + 1, down), has_down, has_up),
        )

    def start(c):
        @pl.when(c[1])
        def _():
            c[0].start()

    def wait_recv(c, target):
        @pl.when(c[2])
        def _():
            c[0].wait_recv()

        @pl.when(jnp.logical_not(c[2]))
        def _():
            target[...] = jnp.zeros(target.shape, target.dtype)

    def wait_send(c):
        @pl.when(c[1])
        def _():
            c[0].wait_send()

    cot_copy = (copy(cot_hbm, cot_next, 0, before), has_before, has_after)
    clip_up, clip_down = exchange(1, clip_hbm.at[:, 0], clip_hbm.at[:, rows - 1], clip_halo, up, down)
    start(clip_up)
    start(clip_down)
    start(cot_copy)

    loads[0].wait()

    def put_act(f, row, values):
        act = activate(values.astype(F32))
        for q, part in enumerate(columns(act)):
            act3[f, row, :, pl.ds(q * ch, ch)] = part

    for f in range(frames):
        for row in range(rows):
            put_act(f, row + 1, clip[f, row])
    wait_recv(clip_up, clip_halo.at[1])
    wait_recv(clip_down, clip_halo.at[0])
    for f in range(frames):
        put_act(f, 0, clip_halo[0, f])
        put_act(f, rows + 1, clip_halo[1, f])

    loads[2].wait()
    total = None
    for r in range(3):
        term = dot(flat(act3[:, r : r + rows]), flat(sw[r]))
        total = term if total is None else total + term
    mid_ext[frames:] = total.astype(BF16).reshape(block)
    mid_copy = (copy(mid, mid_prev, 3, after), has_after, has_before)
    start(mid_copy)

    for r in range(3):
        for f in range(frames):
            act_t[pl.ds(r * ch, ch), pl.ds(f * cells, cells)] = flat(
                act3[f, r : r + rows, :, pl.ds(ch, ch)]
            ).T

    loads[1].wait()
    loads[3].wait()
    wait_recv(cot_copy, cot_next)

    def put_gm(f, row, values):
        shifts = columns(values)
        for q in range(3):
            gm3[f, row, :, pl.ds(q * ch, ch)] = shifts[2 - q]

    total = None
    for k in range(3):
        term = dot(flat(cot_ext[k : k + frames]), tw[k], NT)
        total = term if total is None else total + term
    value = total.astype(BF16).reshape(block)
    gm[...] = value
    gm_up, gm_down = exchange(4, gm.at[:, 0], gm.at[:, rows - 1], gm_halo, up, down)
    start(gm_up)
    start(gm_down)
    for f in range(frames):
        for row in range(rows):
            put_gm(f, row + 1, value[f, row])

    for q in range(3):
        total = dot(act_t[...], flat(gm3[:, 1 : 1 + rows, :, pl.ds(q * ch, ch)]))
        for r in range(3):
            gs[pl.ds((r * 3 + q) * ch, ch), :] = total[r * ch : (r + 1) * ch]

    def turn_mid(t):
        mid_t[:, pl.ds(t * cells, cells)] = flat(mid_ext[t]).T

    def do_temporal():
        for t in range(frames, 2 * frames):
            turn_mid(t)
        wait_recv(mid_copy, mid_prev)
        for t in range(frames):
            turn_mid(t)
        left = jnp.concatenate(
            [mid_t[:, pl.ds((frames - k) * cells, frames * cells)] for k in range(3)], axis=0
        )
        gt[...] = dot(left, flat(cot_ext[:frames]))

    def do_output():
        total = flat(clip[...]).astype(F32)
        for k in range(3):
            total = total + dot(flat(mid_ext[frames - k : 2 * frames - k]), tw[k])
        out[...] = total.astype(BF16).reshape(block)

    def do_gm_halo():
        wait_recv(gm_up, gm_halo.at[1])
        wait_recv(gm_down, gm_halo.at[0])
        for f in range(frames):
            put_gm(f, 0, gm_halo[0, f])
            put_gm(f, rows + 1, gm_halo[1, f])

    def do_grad_act(r):
        total = None
        for q in range(3):
            left = flat(gm3[:, 2 - r : 2 - r + rows, :, pl.ds(q * ch, ch)])
            term = dot(left, sw[r, q], NT)
            total = term if total is None else total + term
        if r == 0:
            grad_act[...] = total
        else:
            grad_act[...] += total

    def do_grad_clip():
        for f in range(frames):
            values = flat(clip[f]).astype(F32)
            scale_inv = lax.rsqrt(jnp.mean(values * values, axis=-1, keepdims=True) + EPSILON)
            normed = values * scale_inv
            gate = 1.0 / (1.0 + jnp.exp(-normed))
            inner = grad_act[pl.ds(f * cells, cells), :] * (gate * (1.0 + normed * (1.0 - gate)))
            slope = scale_inv * (
                inner - normed * jnp.mean(inner * normed, axis=-1, keepdims=True)
            )
            total = flat(cot_ext[f]).astype(F32) + slope
            gclip[f] = total.astype(BF16).reshape(rows, cols, ch)

    scale = 1.0 / math.sqrt(frames * tm_count * rows * h_count * cols)

    if not reduce_inside:
        do_temporal()
        do_output()
        do_gm_halo()
        for r in range(3):
            do_grad_act(r)
        do_grad_clip()
        gs_out[...] = gs[...] * scale
        gt_out[...] = gt[...] * scale
    else:
        rsend, rrecv = rest[-2:]
        bufs = [rest[11 * i : 11 * i + 11] for i in range(len(CHUNKS))]

        def rcopy(src, dst, slot, who):
            return pltpu.make_async_remote_copy(
                src_ref=src, dst_ref=dst, send_sem=rsend.at[slot], recv_sem=rrecv.at[slot],
                device_id=who, device_id_type=MESH,
            )

        def piece(chunk, d):
            kind, first, a, b = chunk
            ref, count = (gs, SPATIAL_ROWS) if kind == "spatial" else (gt, TEMPORAL_ROWS)
            block = ref[pl.ds(pl.multiple_of(d * count, 8), count), :]
            both = jnp.concatenate([block[:, :LANES], block[:, LANES:]], axis=0)
            return both[first : first + a + b]

        def each(count):
            def run(step):
                def four(j, carry):
                    for i in range(4):
                        step(j * 4 + i)
                    return carry

                lax.fori_loop(0, count // 4, four, 0)

            return run

        def owner(j, which):
            return ((j // 8) * 2 + which) * 8 + lax.rem(j, 8)

        def stage_core(i):
            send0, recv0 = bufs[i][:2]

            @each(16)
            def _(j):
                send0[j] = piece(CHUNKS[i], owner(j, 1 - core)).astype(BF16)

            c = rcopy(send0, recv0, 8 * i, by_core)
            c.start()
            return [c]

        def stage_one(i):
            a = CHUNKS[i][2]
            send0, recv0, part, send_a, recv_a, send_b, recv_b = bufs[i][:7]

            @each(16)
            def _(j):
                part[j] = piece(CHUNKS[i], owner(j, core)) + recv0[j].astype(F32)

            @each(8)
            def _(j):
                send_a[j] = part[(1 - xx) * 8 + j, :a].astype(BF16)
                send_b[j] = part[j * 2 + 1 - yy, a:].astype(BF16)

            cs = [
                rcopy(send_a, recv_a, 8 * i + 1, by_x),
                rcopy(send_b, recv_b, 8 * i + 2, by_y),
            ]
            for c in cs:
                c.start()
            return cs

        def stage_two(i):
            a = CHUNKS[i][2]
            part, _, recv_a, _, recv_b, send_a2, recv_a2, send_b2, recv_b2 = bufs[i][2:11]

            @each(4)
            def _(j):
                away = j * 2 + 1 - yy
                send_a2[j] = (part[xx * 8 + away, :a] + recv_a[away].astype(F32)).astype(BF16)
                far = (1 - xx) * 4 + j
                send_b2[j] = (part[far * 2 + yy, a:] + recv_b[far].astype(F32)).astype(BF16)

            cs = [
                rcopy(send_a2, recv_a2, 8 * i + 3, by_y),
                rcopy(send_b2, recv_b2, 8 * i + 4, by_x),
            ]
            for c in cs:
                c.start()
            return cs

        z_bufs = rest[11 * len(CHUNKS) : -2]

        def stage_z(i):
            a = CHUNKS[i][2]
            part, _, recv_a, _, recv_b, _, recv_a2, _, recv_b2 = bufs[i][2:11]
            total_z, send_z, recv_z = z_bufs[3 * i : 3 * i + 3]

            @each(4)
            def _(j):
                near = j * 2 + yy
                first = part[xx * 8 + near, :a] + recv_a[near].astype(F32) + recv_a2[j].astype(F32)
                last = (
                    part[xx * 8 + near, a:] + recv_b[xx * 4 + j].astype(F32) + recv_b2[j].astype(F32)
                )
                value = jnp.concatenate([first, last], axis=0)
                total_z[j] = value
                send_z[j] = value.astype(BF16)

            cs = [
                rcopy(
                    send_z.at[lax.rem(zz + off, 4)], recv_z.at[off - 1], 8 * i + 4 + off, by_z[off - 1]
                )
                for off in (1, 2, 3)
            ]
            for c in cs:
                c.start()
            return cs

        def final(i):
            total_z, _, recv_z = z_bufs[3 * i : 3 * i + 3]
            value = total_z[zz]
            for off in range(3):
                value = value + recv_z[off].astype(F32)
            return value * scale

        def finish(copies):
            for c in copies:
                c.wait()

        def place(ref, value, count):
            ref[pl.ds(0, count, stride=2), :] = value[:count]
            ref[pl.ds(1, count, stride=2), :] = value[count:]

        spatial = (0, 1)
        flight = {i: stage_core(i) for i in spatial}
        do_temporal()
        flight[2] = stage_core(2)

        def advance(stage):
            for i in range(len(CHUNKS)):
                finish(flight[i])
                flight[i] = stage(i)

        advance(stage_one)
        do_output()
        do_gm_halo()
        do_grad_act(0)
        advance(stage_two)
        do_grad_act(1)
        advance(stage_z)
        do_grad_act(2)
        do_grad_clip()
        done = []
        for i in range(len(CHUNKS)):
            finish(flight[i])
            done.append(final(i))
        place(gs_out, jnp.concatenate(done[:2], axis=0), SPATIAL_ROWS)
        place(gt_out, done[2], TEMPORAL_ROWS)

    for c in (clip_up, clip_down, cot_copy, mid_copy, gm_up, gm_down):
        wait_send(c)


def hand_on(*refs):
    count = len(refs) // 2
    copies = [
        pltpu.make_async_copy(refs[i], refs[count + i], refs[-1].at[i]) for i in range(count)
    ]
    for c in copies:
        c.start()
    for c in copies:
        c.wait()


def handed_on(*arrays):
    place = pl.BlockSpec(memory_space=pltpu.HBM)
    return pl.pallas_call(
        hand_on,
        out_shape=tuple(jax.ShapeDtypeStruct(x.shape, x.dtype) for x in arrays),
        in_specs=[pl.BlockSpec(memory_space=pltpu.VMEM)] * len(arrays),
        out_specs=(place,) * len(arrays),
        scratch_shapes=[pltpu.SemaphoreType.DMA((len(arrays),))],
        compiler_params=pltpu.CompilerParams(vmem_limit_bytes=4 * 1024 * 1024),
        name="hand_on",
    )(*arrays)


def shards(sizes, clip, cot, sw, tw):
    tm_count, h_count = sizes
    frames, rows, cols, ch = clip.shape
    inside = sizes == (4, 8) and ch == 256 and frames == 2
    wide = (frames, rows + 2, cols, 3 * ch)
    edge = (2, frames, cols, ch)
    vmem = pl.BlockSpec(memory_space=pltpu.VMEM)
    scratch = [pltpu.VMEM(x.shape, x.dtype) for x in (clip, sw, tw)]
    scratch += [
        pltpu.SemaphoreType.DMA((4,)),
        pltpu.VMEM(edge, BF16),
        pltpu.VMEM((2 * frames, rows, cols, ch), BF16),
        pltpu.VMEM((2 * frames, rows, cols, ch), BF16),
        pltpu.VMEM((ch, 2 * frames * rows * cols), BF16),
        pltpu.VMEM(clip.shape, BF16),
        pltpu.VMEM(edge, BF16),
        pltpu.VMEM(wide, BF16),
        pltpu.VMEM(wide, BF16),
        pltpu.VMEM((3 * ch, frames * rows * cols), BF16),
        pltpu.VMEM((frames * rows * cols, ch), F32),
        pltpu.VMEM((9 * ch, ch), F32),
        pltpu.VMEM((3 * ch, ch), F32),
        pltpu.SemaphoreType.DMA((6,)),
        pltpu.SemaphoreType.DMA((6,)),
    ]
    gs_shape, gt_shape = (9 * ch, ch), (3 * ch, ch)
    if inside:
        gs_shape, gt_shape = (2 * SPATIAL_ROWS, LANES), (2 * TEMPORAL_ROWS, LANES)
        for _, _, a, b in CHUNKS:
            n = a + b
            scratch += [pltpu.VMEM((16, n, LANES), BF16)] * 2
            scratch += [pltpu.VMEM((16, n, LANES), F32)]
            scratch += [pltpu.VMEM((8, a, LANES), BF16)] * 2
            scratch += [pltpu.VMEM((8, b, LANES), BF16)] * 2
            scratch += [pltpu.VMEM((4, a, LANES), BF16)] * 2
            scratch += [pltpu.VMEM((4, b, LANES), BF16)] * 2
        for _, _, a, b in CHUNKS:
            n = a + b
            scratch += [
                pltpu.VMEM((4, n, LANES), F32),
                pltpu.VMEM((4, n, LANES), BF16),
                pltpu.VMEM((3, n, LANES), BF16),
            ]
        scratch += [pltpu.SemaphoreType.DMA((8 * len(CHUNKS),))] * 2
    out, gclip, gs, gt = pl.pallas_call(
        functools.partial(body, sizes, inside),
        out_shape=(
            jax.ShapeDtypeStruct(clip.shape, BF16),
            jax.ShapeDtypeStruct(clip.shape, BF16),
            jax.ShapeDtypeStruct(gs_shape, F32),
            jax.ShapeDtypeStruct(gt_shape, F32),
        ),
        in_specs=[pl.BlockSpec(memory_space=pltpu.HBM)] * 4,
        out_specs=(vmem,) * 4,
        scratch_shapes=scratch,
        compiler_params=pltpu.CompilerParams(
            collective_id=0, has_side_effects=True, vmem_limit_bytes=531 * 1024 * 1024 // 10
        ),
        name="section",
    )(clip, cot, sw, tw)
    if inside:
        out, gclip, gs, gt = handed_on(out, gclip, gs, gt)
    gs, gt = gs.reshape(-1), gt.reshape(-1)
    if not inside:
        gs, gt = (
            lax.psum_scatter(gs, ("tm", "height"), scatter_dimension=0, tiled=True),
            lax.psum_scatter(gt, ("tm", "height"), scatter_dimension=0, tiled=True),
        )
    return out, gclip, gs, gt


def solution(mesh):
    sizes = (mesh.shape["tm"], mesh.shape["height"])
    return jax.shard_map(
        functools.partial(shards, sizes),
        mesh=mesh,
        in_specs=(P("tm", "height", None, None), P("tm", "height", None, None), P(), P()),
        out_specs=(
            P("tm", "height", None, None),
            P("tm", "height", None, None),
            P(("tm", "height")),
            P(("tm", "height")),
        ),
        check_vma=False,
    )
```
